512 devices in a mesh: head: 32 (over z_lo, y, core), seq: 16 (over z_hi, x).
Axes of the slice: x: 4, y: 4, z: 16 (z_hi: 4, z_lo: 4; z = z_hi * 4 + z_lo), core: 2. Of those that a mesh axis runs over, the one named last changes fastest.
Arguments:
- query_rows: bfloat16 [2048, 16384], P('seq', 'head'), may hold values from -512 to 512
- key_rows: bfloat16 [2048, 1024], P('seq'), may hold values from -32 to 32
- value_rows: bfloat16 [2048, 1024], P('seq'), may hold values from -6 to 6
- positions: int32 [2048], P('seq'), may hold values from 0 to 511, as said below
Outputs:
- attended: bfloat16 [2048, 16384], P('seq', 'head')
- hessian: float32 [16384, 16384], P('head', 'seq')
The draws below stay inside these ranges and needn't reach their ends.
Inputs may be any that keep to these rules, and one draw needn't show every extreme that they name: Each aligned block of 4 spans of 128 tokens is one sequence; each span holds 128 consecutive ascending positions starting at a multiple of 128, and the sequence's spans together hold every position 0 to 511 once.
All inputs are finite; a program needn't handle non-finite values.
Results may differ from the reference program's by a relative error of at most 0.0037.
Values may be sent and summed in bfloat16 or wider, within the bound.
No kernel may reach another device: no remote copies, remote signals or barrier semaphores. Data moves between devices by JAX's collectives and lax.ppermute only.
A program may use at most 64 MiB of HBM per device.

```python
import jax
import jax.numpy as jnp
from jax import lax

HEADS = 128
KVH = 8
HD = 128
TOK_DEV = 128
SPANS = 4
LENGTH = 512
TOKENS = 2048


def draw_key_rows(key, part):
    noise_key = jax.random.fold_in(key, 1)
    drawn = jnp.clip(jax.random.normal(noise_key, (TOKENS, KVH * HD), jnp.float32), -4.0, 4.0)
    return drawn.astype(jnp.bfloat16)


def draw_query_rows(key, part):
    noise_key = jax.random.fold_in(key, 2)
    drawn = jnp.clip(jax.random.normal(noise_key, (TOKENS, HEADS * HD), jnp.float32), -4.0, 4.0)
    return drawn.astype(jnp.bfloat16)


def draw_positions(key, part):
    sequence_keys = jax.random.split(jax.random.fold_in(key, 5), TOKENS // LENGTH)
    slots = jax.vmap(lambda single: jax.random.permutation(single, SPANS))(sequence_keys)
    within = jnp.arange(TOK_DEV, dtype=jnp.int32)
    return (slots[:, :, None].astype(jnp.int32) * TOK_DEV + within[None, None, :]).reshape(TOKENS)


def shard_levels(own_key, shape, shards, least, largest):
    level = 1.0
    for position, shards_of in shards:
        steps = jax.random.uniform(jax.random.fold_in(jax.random.fold_in(own_key, 6), position), (shards_of,), jnp.float32, least / len(shards), largest / len(shards))
        level = level * jnp.repeat(jnp.exp(steps), shape[position] // shards_of).reshape((-1,) + (1,) * (len(shape) - 1 - position))
    return level


def noise(rng, dims, spread, limit, cuts=(), kind=jnp.bfloat16):
    entries = jax.random.normal(rng, dims, jnp.float32) * spread
    if len(cuts) > 0:
        entries = shard_levels(rng, dims, cuts, -0.22, 0.18) * entries
    return jnp.clip(entries, min=-limit, max=limit).astype(kind)


def setup_inputs(seed: int = 0) -> dict:
    splits = jax.random.split(jax.random.key(seed), 5)
    query_rows = draw_query_rows(jax.random.fold_in(splits[4], 71), 0)
    key_rows = draw_key_rows(jax.random.fold_in(splits[4], 71), 0)
    value_rows = noise(splits[2], (TOKENS, KVH * HD), 1.0, 6.0, ((0, 16),))
    positions = draw_positions(jax.random.fold_in(splits[4], 71), 0)
    return {"query_rows": query_rows, "key_rows": key_rows, "value_rows": value_rows, "positions": positions}


def reference(query_rows, key_rows, value_rows, positions):
    group_size = HEADS // KVH
    sequence_count = TOKENS // LENGTH
    score_scale = HD ** -0.5
    queries = query_rows.reshape(sequence_count, LENGTH, KVH, group_size, HD)
    queries = jnp.transpose(queries, (0, 2, 3, 1, 4)).reshape(sequence_count, KVH, group_size * LENGTH, HD)
    key_heads = jnp.transpose(key_rows.reshape(sequence_count, LENGTH, KVH, HD), (0, 2, 1, 3))
    value_heads = jnp.transpose(value_rows.reshape(sequence_count, LENGTH, KVH, HD), (0, 2, 1, 3))
    places = positions.reshape(sequence_count, LENGTH)

    def head_group(inputs):
        query_block, key_block, value_block, visible = inputs
        scores = jnp.dot(query_block, key_block.T, preferred_element_type=jnp.float32) * score_scale
        scores = scores.reshape(group_size, LENGTH, LENGTH)
        masked = jnp.where(visible[None], scores, -jnp.inf)
        row_top = jnp.max(masked, axis=2, keepdims=True)
        weights = jnp.exp(masked - row_top)
        weight_sum = jnp.sum(weights, axis=2, keepdims=True)
        mixed = jnp.dot(weights.astype(jnp.bfloat16).reshape(group_size * LENGTH, LENGTH), value_block,
                        preferred_element_type=jnp.float32)
        return (mixed.reshape(group_size, LENGTH, HD) / weight_sum).astype(jnp.bfloat16)

    def sequence_part(inputs):
        query_seq, key_seq, value_seq, place_seq = inputs
        visible = place_seq[None, :] <= place_seq[:, None]
        visible_all = jnp.broadcast_to(visible, (KVH, LENGTH, LENGTH))
        return lax.map(head_group, (query_seq, key_seq, value_seq, visible_all))

    outputs = lax.map(sequence_part, (queries, key_heads, value_heads, places))
    attended = jnp.transpose(outputs, (0, 3, 1, 2, 4)).reshape(TOKENS, HEADS * HD)
    hessian = jnp.dot(attended.T, attended, preferred_element_type=jnp.float32)
    return attended, hessian
```

```python
import jax
import jax.numpy as jnp
from jax import lax
from jax.experimental import pallas as pl
from jax.experimental.pallas import tpu as pltpu
from jax.sharding import Mesh
from jax.sharding import PartitionSpec as P

HEADS = 128
KVH = 8
HD = 128
RING = 4
AXES = ("zl", "y", "core", "zh", "x")
HEAD = ("zl", "y", "core")
SEQ = ("zh", "x")
VMEM = 48 * 1024 * 1024


def pack_kernel(g_ref, k_ref, v_ref, p_ref, o_ref):
    tok = k_ref.shape[0]
    o_ref[:tok] = k_ref[...]
    o_ref[tok : 2 * tok] = v_ref[...]
    p = p_ref[...]
    high = p >> 7
    row = lax.broadcasted_iota(jnp.int32, (16, tok), 0)
    both = jnp.where(row == 0, high, p - (high << 7))
    o_ref[2 * tok :] = both.astype(jnp.float32).astype(jnp.bfloat16)


def pack(key_head, key_rows, value_rows, positions):
    tok = key_rows.shape[0]
    return pl.pallas_call(
        pack_kernel,
        out_shape=jax.ShapeDtypeStruct((2 * tok + 16, HD), jnp.bfloat16),
        grid_spec=pltpu.PrefetchScalarGridSpec(
            num_scalar_prefetch=1,
            grid=(1,),
            in_specs=[
                pl.BlockSpec((tok, HD), lambda i, g: (0, g[0])),
                pl.BlockSpec((tok, HD), lambda i, g: (0, g[0])),
                pl.BlockSpec((1, tok), lambda i, g: (0, 0)),
            ],
            out_specs=pl.BlockSpec((2 * tok + 16, HD), lambda i, g: (0, 0)),
        ),
        name="pack",
    )(key_head, key_rows, value_rows, positions.reshape(1, tok))


def attend_kernel(q_ref, kv_ref, p_ref, o_ref):
    tok, width = q_ref.shape
    spans = kv_ref.shape[0]
    keys = jnp.concatenate([kv_ref[s, :tok, :] for s in range(spans)], axis=0)
    values = jnp.concatenate([kv_ref[s, tok : 2 * tok, :] for s in range(spans)], axis=0)
    places = []
    for s in range(spans):
        both = kv_ref[s, 2 * tok :, :].astype(jnp.float32)
        places.append(both[0:1] * 128.0 + both[1:2])
    place = jnp.concatenate(places, axis=1)
    own = p_ref[...].astype(jnp.float32)
    visible = place <= own
    for h in range(width // HD):
        q = q_ref[:, h * HD : (h + 1) * HD]
        scores = lax.dot_general(
            q, keys, (((1,), (1,)), ((), ())), preferred_element_type=jnp.float32
        ) * (HD ** (-0.5))
        masked = jnp.where(visible, scores, -jnp.inf)
        top = jnp.max(masked, axis=1, keepdims=True)
        weights = jnp.exp(masked - top)
        total = jnp.sum(weights, axis=1, keepdims=True)
        mixed = jnp.dot(weights.astype(jnp.bfloat16), values, preferred_element_type=jnp.float32)
        o_ref[:, h * HD : (h + 1) * HD] = (mixed / total).astype(jnp.bfloat16)


def attend(queries, gathered, positions):
    tok, width = queries.shape
    return pl.pallas_call(
        attend_kernel,
        out_shape=jax.ShapeDtypeStruct((tok, width), jnp.bfloat16),
        compiler_params=pltpu.CompilerParams(vmem_limit_bytes=VMEM),
        name="attend",
    )(queries, gathered, positions.reshape(tok, 1))


def hessian_kernel(s_ref, r_ref, a_ref, b_ref, o_ref):
    step = pl.program_id(0)
    core = s_ref[1]
    half = a_ref.shape[2]
    contract = (((0,), (0,)), ((), ()))
    rows = r_ref[0]
    for which, ref in ((core, a_ref), (1 - core, b_ref)):
        part = lax.dot_general(rows, ref[0], contract, preferred_element_type=jnp.float32)
        cols = pl.ds(pl.multiple_of(which * half, half), half)

        @pl.when(step == 0)
        def _():
            o_ref[:, cols] = part

        @pl.when(step > 0)
        def _():
            o_ref[:, cols] += part


def hessian_of(scalars, rows, own, other):
    steps, depth, width = rows.shape
    half = own.shape[2]
    turned = lambda i, s: ((i + s[0]) & (RING - 1), 0, 0)
    return pl.pallas_call(
        hessian_kernel,
        out_shape=jax.ShapeDtypeStruct((width, 2 * half), jnp.float32),
        grid_spec=pltpu.PrefetchScalarGridSpec(
            num_scalar_prefetch=1,
            grid=(steps,),
            in_specs=[
                pl.BlockSpec((1, depth, width), lambda i, s: (i, 0, 0)),
                pl.BlockSpec((1, depth, half), turned),
                pl.BlockSpec((1, depth, half), turned),
            ],
            out_specs=pl.BlockSpec((width, 2 * half), lambda i, s: (0, 0)),
        ),
        compiler_params=pltpu.CompilerParams(vmem_limit_bytes=VMEM),
        name="hessian",
    )(scalars, rows, own, other)


def shift(value, axis, by):
    return lax.ppermute(value, axis, [(i, (i + by) % RING) for i in range(RING)])


def ring(value, axis):
    half = value.shape[0] // 2
    after = shift(value, axis, -1)
    before = shift(value, axis, 1)
    first = shift(after[:half], axis, -1)
    second = shift(before[half:], axis, 1)
    return jnp.stack([value, after, jnp.concatenate([first, second]), before])


def swap(value):
    pairs = []
    for chip in range(16):
        for core in range(2):
            for span in range(16):
                pairs.append(((chip * 2 + core) * 16 + span, (span * 2 + core) * 16 + chip))
    return lax.ppermute(value, HEAD + SEQ, pairs)


def on_device(query_rows, key_rows, value_rows, positions):
    tok = query_rows.shape[0]
    local_heads = query_rows.shape[1] // HD
    head = lax.axis_index(HEAD)
    key_head = (head * local_heads // (HEADS // KVH)).astype(jnp.int32).reshape(1)
    packed = pack(key_head, key_rows, value_rows, positions)
    gathered = lax.all_gather(packed, "x", axis=0)
    attended = attend(query_rows, gathered, positions)
    chunk = swap(attended)
    rows = lax.all_gather(attended, "zh", axis=0, tiled=True)
    cols = lax.all_gather(chunk, "zl", axis=0, tiled=True)
    own = ring(cols, "y")
    rows = ring(rows, "x")
    other = lax.ppermute(own, "core", [(0, 1), (1, 0)])
    turn = (lax.axis_index("x") - lax.axis_index("y")) & (RING - 1)
    scalars = jnp.stack([turn, lax.axis_index("core")]).astype(jnp.int32)
    return attended, hessian_of(scalars, rows, own, other)


def solution(mesh):
    fine = Mesh(mesh.devices.reshape(4, 4, 2, 4, 4), AXES)
    placed = (P(SEQ, HEAD), P(SEQ, None), P(SEQ, None), P(SEQ))
    return jax.shard_map(
        on_device,
        mesh=fine,
        in_specs=placed,
        out_specs=(P(SEQ, HEAD), P(HEAD, SEQ)),
        check_vma=False,
    )
```

```python
import jax
import jax.numpy as jnp
from jax import lax
from jax.experimental import pallas as pl
from jax.experimental.pallas import tpu as pltpu
from jax.sharding import Mesh
from jax.sharding import PartitionSpec as P

HEADS = 128
KVH = 8
HD = 128
RING = 4
AXES = ("zl", "y", "core", "zh", "x")
HEAD = ("zl", "y", "core")
SEQ = ("zh", "x")
VMEM = 48 * 1024 * 1024


def pack_kernel(g_ref, k_ref, v_ref, p_ref, o_ref):
    tok = k_ref.shape[0]
    o_ref[:tok] = k_ref[...]
    o_ref[tok : 2 * tok] = v_ref[...]
    p = p_ref[...]
    high = p >> 7
    row = lax.broadcasted_iota(jnp.int32, (16, tok), 0)
    both = jnp.where(row == 0, high, p - (high << 7))
    o_ref[2 * tok :] = both.astype(jnp.float32).astype(jnp.bfloat16)


def pack(key_head, key_rows, value_rows, positions):
    tok = key_rows.shape[0]
    return pl.pallas_call(
        pack_kernel,
        out_shape=jax.ShapeDtypeStruct((2 * tok + 16, HD), jnp.bfloat16),
        grid_spec=pltpu.PrefetchScalarGridSpec(
            num_scalar_prefetch=1,
            grid=(1,),
            in_specs=[
                pl.BlockSpec((tok, HD), lambda i, g: (0, g[0])),
                pl.BlockSpec((tok, HD), lambda i, g: (0, g[0])),
                pl.BlockSpec((1, tok), lambda i, g: (0, 0)),
            ],
            out_specs=pl.BlockSpec((2 * tok + 16, HD), lambda i, g: (0, 0)),
        ),
        name="pack",
    )(key_head, key_rows, value_rows, positions.reshape(1, tok))


def attend_kernel(q_ref, kv_ref, p_ref, o_ref):
    tok, width = q_ref.shape
    spans = kv_ref.shape[0]
    keys = jnp.concatenate([kv_ref[s, :tok, :] for s in range(spans)], axis=0)
    values = jnp.concatenate([kv_ref[s, tok : 2 * tok, :] for s in range(spans)], axis=0)
    places = []
    for s in range(spans):
        both = kv_ref[s, 2 * tok :, :].astype(jnp.float32)
        places.append(both[0:1] * 128.0 + both[1:2])
    place = jnp.concatenate(places, axis=1)
    own = p_ref[...].astype(jnp.float32)
    visible = place <= own
    for h in range(width // HD):
        q = q_ref[:, h * HD : (h + 1) * HD]
        scores = lax.dot_general(
            q, keys, (((1,), (1,)), ((), ())), preferred_element_type=jnp.float32
        ) * (HD ** (-0.5))
        masked = jnp.where(visible, scores, -jnp.inf)
        top = jnp.max(masked, axis=1, keepdims=True)
        weights = jnp.exp(masked - top)
        total = jnp.sum(weights, axis=1, keepdims=True)
        mixed = jnp.dot(weights.astype(jnp.bfloat16), values, preferred_element_type=jnp.float32)
        o_ref[:, h * HD : (h + 1) * HD] = (mixed / total).astype(jnp.bfloat16)


def attend(queries, gathered, positions):
    tok, width = queries.shape
    return pl.pallas_call(
        attend_kernel,
        out_shape=jax.ShapeDtypeStruct((tok, width), jnp.bfloat16),
        compiler_params=pltpu.CompilerParams(vmem_limit_bytes=VMEM),
        name="attend",
    )(queries, gathered, positions.reshape(tok, 1))


def hessian_kernel(s_ref, r_ref, a_ref, b_ref, o_ref):
    step = pl.program_id(0)
    core = s_ref[1]
    half = a_ref.shape[2]
    contract = (((0,), (0,)), ((), ()))
    rows = r_ref[0]
    for which, ref in ((core, a_ref), (1 - core, b_ref)):
        part = lax.dot_general(rows, ref[0], contract, preferred_element_type=jnp.float32)
        cols = pl.ds(pl.multiple_of(which * half, half), half)

        @pl.when(step == 0)
        def _():
            o_ref[:, cols] = part

        @pl.when(step > 0)
        def _():
            o_ref[:, cols] += part


def hessian_of(scalars, rows, own, other):
    steps, depth, width = rows.shape
    half = own.shape[2]
    turned = lambda i, s: ((i + s[0]) & (RING - 1), 0, 0)
    return pl.pallas_call(
        hessian_kernel,
        out_shape=jax.ShapeDtypeStruct((width, 2 * half), jnp.float32),
        grid_spec=pltpu.PrefetchScalarGridSpec(
            num_scalar_prefetch=1,
            grid=(steps,),
            in_specs=[
                pl.BlockSpec((1, depth, width), lambda i, s: (i, 0, 0)),
                pl.BlockSpec((1, depth, half), turned),
                pl.BlockSpec((1, depth, half), turned),
            ],
            out_specs=pl.BlockSpec((width, 2 * half), lambda i, s: (0, 0)),
        ),
        compiler_params=pltpu.CompilerParams(vmem_limit_bytes=VMEM),
        name="hessian",
    )(scalars, rows, own, other)


def shift(value, axis, by):
    return lax.ppermute(value, axis, [(i, (i + by) % RING) for i in range(RING)])


def neighbours(value, axis):
    return shift(value, axis, -1), shift(value, axis, 1)


def opposite(after, before, axis):
    half = after.shape[0] // 2
    first = shift(after[:half], axis, -1)
    second = shift(before[half:], axis, 1)
    return jnp.concatenate([first, second])


def spread(value, axis):
    copies = jnp.broadcast_to(value[None], (RING,) + value.shape)
    return lax.all_to_all(copies, axis, split_axis=0, concat_axis=0, tiled=True)


def swap(value):
    pairs = []
    for chip in range(16):
        for core in range(2):
            for span in range(16):
                pairs.append(((chip * 2 + core) * 16 + span, (span * 2 + core) * 16 + chip))
    return lax.ppermute(value, HEAD + SEQ, pairs)


def on_device(query_rows, key_rows, value_rows, positions):
    tok = query_rows.shape[0]
    local_heads = query_rows.shape[1] // HD
    head = lax.axis_index(HEAD)
    key_head = (head * local_heads // (HEADS // KVH)).astype(jnp.int32).reshape(1)
    packed = pack(key_head, key_rows, value_rows, positions)
    gathered = spread(packed, "x")
    attended = attend(query_rows, gathered, positions)
    chunk = swap(attended)
    rows = lax.all_gather(attended, "zh", axis=0, tiled=True)
    chunk, rows = lax.optimization_barrier((chunk, rows))
    cols = spread(chunk, "zl").reshape(RING * tok, -1)
    after, before = neighbours(rows, "x")
    cols, after, before = lax.optimization_barrier((cols, after, before))
    across = opposite(after, before, "x")
    own = spread(cols, "y")
    own, across = lax.optimization_barrier((own, across))
    rows = jnp.stack([rows, after, across, before])
    other = lax.ppermute(own, "core", [(0, 1), (1, 0)])
    scalars = jnp.stack([lax.axis_index("x"), lax.axis_index("core")]).astype(jnp.int32)
    return attended, hessian_of(scalars, rows, own, other)


def solution(mesh):
    fine = Mesh(mesh.devices.reshape(4, 4, 2, 4, 4), AXES)
    placed = (P(SEQ, HEAD), P(SEQ, None), P(SEQ, None), P(SEQ))
    return jax.shard_map(
        on_device,
        mesh=fine,
        in_specs=placed,
        out_specs=(P(SEQ, HEAD), P(HEAD, SEQ)),
        check_vma=False,
    )
```

```python
import functools

import jax
import jax.numpy as jnp
from jax import lax
from jax.experimental import pallas as pl
from jax.experimental.pallas import tpu as pltpu
from jax.sharding import Mesh
from jax.sharding import PartitionSpec as P

HEADS = 128
KVH = 8
HD = 128
RING = 4
AXES = ("zl", "y", "core", "zh", "x")
HEAD = ("zl", "y", "core")
SEQ = ("zh", "x")
VMEM = 24 * 1024 * 1024


def pack_kernel(g_ref, k_ref, v_ref, p_ref, o_ref):
    tok = k_ref.shape[0]
    p = p_ref[...]
    high = p >> 7
    row = lax.broadcasted_iota(jnp.int32, (16, tok), 0)
    both = jnp.where(row == 0, high, p - (high << 7))
    both = both.astype(jnp.float32).astype(jnp.bfloat16)
    for copy in range(o_ref.shape[0]):
        o_ref[copy, :tok] = k_ref[...]
        o_ref[copy, tok : 2 * tok] = v_ref[...]
        o_ref[copy, 2 * tok :] = both


def pack(key_head, key_rows, value_rows, positions):
    tok = key_rows.shape[0]
    return pl.pallas_call(
        pack_kernel,
        out_shape=jax.ShapeDtypeStruct((RING, 2 * tok + 16, HD), jnp.bfloat16),
        grid_spec=pltpu.PrefetchScalarGridSpec(
            num_scalar_prefetch=1,
            grid=(1,),
            in_specs=[
                pl.BlockSpec((tok, HD), lambda i, g: (0, g[0])),
                pl.BlockSpec((tok, HD), lambda i, g: (0, g[0])),
                pl.BlockSpec((1, tok), lambda i, g: (0, 0)),
            ],
            out_specs=pl.BlockSpec((RING, 2 * tok + 16, HD), lambda i, g: (0, 0, 0)),
        ),
        name="pack",
    )(key_head, key_rows, value_rows, positions.reshape(1, tok))


def attend_kernel(q_ref, kv_ref, p_ref, o_ref):
    heads, tok, _ = q_ref.shape
    spans = kv_ref.shape[0]
    keys = jnp.concatenate([kv_ref[s, :tok, :] for s in range(spans)], axis=0)
    values = jnp.concatenate([kv_ref[s, tok : 2 * tok, :] for s in range(spans)], axis=0)
    places = []
    for s in range(spans):
        both = kv_ref[s, 2 * tok :, :].astype(jnp.float32)
        places.append(both[0:1] * 128.0 + both[1:2])
    place = jnp.concatenate(places, axis=1)
    own = p_ref[...].astype(jnp.float32)
    visible = place <= own
    for h in range(heads):
        q = q_ref[h]
        scores = lax.dot_general(
            q, keys, (((1,), (1,)), ((), ())), preferred_element_type=jnp.float32
        ) * (HD ** (-0.5))
        masked = jnp.where(visible, scores, -jnp.inf)
        top = jnp.max(masked, axis=1, keepdims=True)
        weights = jnp.exp(masked - top)
        total = jnp.sum(weights, axis=1, keepdims=True)
        mixed = jnp.dot(weights.astype(jnp.bfloat16), values, preferred_element_type=jnp.float32)
        o_ref[:, h * HD : (h + 1) * HD] = (mixed / total).astype(jnp.bfloat16)


def attend(queries, gathered, positions):
    heads, tok, _ = queries.shape
    return pl.pallas_call(
        attend_kernel,
        out_shape=jax.ShapeDtypeStruct((tok, heads * HD), jnp.bfloat16),
        compiler_params=pltpu.CompilerParams(vmem_limit_bytes=VMEM),
        name="attend",
    )(queries, gathered, positions.reshape(tok, 1))


CONTRACT = (((0,), (0,)), ((), ()))


def product_kernel(final, s_ref, one_ref, two_ref, *rest):
    o_ref = rest[-1]
    core = s_ref[0]

    def product(left, right):
        depth = left.shape[0] * left.shape[1]
        o_ref[...] = lax.dot_general(
            left[...].reshape(depth, left.shape[2]),
            right[...].reshape(depth, right.shape[2]),
            CONTRACT,
            preferred_element_type=jnp.float32,
        )

    @pl.when(core == 0)
    def _():
        product(one_ref, rest[0] if final else two_ref)

    @pl.when(core == 1)
    def _():
        product(two_ref, rest[1] if final else one_ref)


def hessian_half(core, operands, filled=None):
    width = operands[0].shape[2]
    final = filled is not None
    whole = [pl.BlockSpec(v.shape, lambda i, s: (0, 0, 0)) for v in operands]
    args = [core, *operands]
    aliases = {}
    if final:
        aliases = {len(args): 0}
        whole.append(pl.BlockSpec(memory_space=pl.ANY))
        args.append(filled)
    return pl.pallas_call(
        functools.partial(product_kernel, final),
        out_shape=jax.ShapeDtypeStruct((width, 2 * width), jnp.float32),
        grid_spec=pltpu.PrefetchScalarGridSpec(
            num_scalar_prefetch=1,
            grid=(1,),
            in_specs=whole,
            out_specs=pl.BlockSpec(
                (width, width), lambda i, s: (0, 1 - s[0] if final else s[0])
            ),
        ),
        input_output_aliases=aliases,
        compiler_params=pltpu.CompilerParams(vmem_limit_bytes=VMEM),
        name="hessian_half",
    )(*args)


PLANE = ("y", "core", "x")


def mixed_groups(along_x):
    place = lambda y, core, x: (y * 2 + core) * RING + x
    groups = [[place(y, along_x, x) for x in range(RING)] for y in range(RING)]
    return groups + [[place(y, 1 - along_x, x) for y in range(RING)] for x in range(RING)]


def exchange_plane(value, along_x):
    return lax.all_to_all(value, PLANE, 0, 0, axis_index_groups=mixed_groups(along_x), tiled=True)


def swap_cores(value):
    return lax.ppermute(value, "core", [(0, 1), (1, 0)])


def copies(value):
    return jnp.broadcast_to(value[None], (RING,) + value.shape)


def exchange(value, axis):
    return lax.all_to_all(value, axis, split_axis=0, concat_axis=0, tiled=True)


def swap(value):
    pairs = []
    for chip in range(16):
        for core in range(2):
            for span in range(16):
                pairs.append(((chip * 2 + core) * 16 + span, (span * 2 + core) * 16 + chip))
    return lax.ppermute(value, HEAD + SEQ, pairs)


def on_device(query_rows, key_rows, value_rows, positions):
    tok = query_rows.shape[0]
    local_heads = query_rows.shape[1] // HD
    head = lax.axis_index(HEAD)
    key_head = (head * local_heads // (HEADS // KVH)).astype(jnp.int32).reshape(1)
    packed = pack(key_head, key_rows, value_rows, positions)
    gathered = exchange(packed, "x")
    queries = jnp.transpose(query_rows.reshape(tok, local_heads, HD), (1, 0, 2))
    attended = attend(queries, gathered, positions)
    chunk = swap(attended)
    chunk, mine = lax.optimization_barrier((chunk, attended))
    cols = exchange(copies(chunk), "zl").reshape(RING * tok, -1)
    rows = lax.all_gather(mine, "zh", axis=0, tiled=True)
    cols, rows = lax.optimization_barrier((cols, rows))
    core = lax.axis_index("core")
    one = exchange_plane(copies(jnp.where(core == 0, rows, cols)), 0)
    later = copies(jnp.where(core == 0, cols, rows))
    one, later = lax.optimization_barrier((one, later))
    one_across = swap_cores(one)
    two = exchange_plane(later, 1)
    two, one_across = lax.optimization_barrier((two, one_across))
    two_across = swap_cores(two)
    core = core.astype(jnp.int32).reshape(1)
    hessian = hessian_half(core, (one, two))
    hessian = hessian_half(core, (one, two, one_across, two_across), hessian)
    return attended, hessian


def solution(mesh):
    fine = Mesh(mesh.devices.reshape(4, 4, 2, 4, 4), AXES)
    placed = (P(SEQ, HEAD), P(SEQ, None), P(SEQ, None), P(SEQ))
    return jax.shard_map(
        on_device,
        mesh=fine,
        in_specs=placed,
        out_specs=(P(SEQ, HEAD), P(HEAD, SEQ)),
        check_vma=False,
    )
```

```python
import jax
import jax.numpy as jnp
from jax import lax
from jax.experimental import pallas as pl
from jax.experimental.pallas import tpu as pltpu
from jax.sharding import Mesh
from jax.sharding import PartitionSpec as P

HEADS = 128
KVH = 8
HD = 128
RING = 4
AXES = ("zl", "y", "core", "zh", "x")
HEAD = ("zl", "y", "core")
SEQ = ("zh", "x")
VMEM = 24 * 1024 * 1024


def pack_kernel(g_ref, k_ref, v_ref, p_ref, o_ref):
    tok = k_ref.shape[0]
    p = p_ref[...]
    high = p >> 7
    row = lax.broadcasted_iota(jnp.int32, (16, tok), 0)
    both = jnp.where(row == 0, high, p - (high << 7))
    both = both.astype(jnp.float32).astype(jnp.bfloat16)
    for copy in range(o_ref.shape[0]):
        o_ref[copy, :tok] = k_ref[...]
        o_ref[copy, tok : 2 * tok] = v_ref[...]
        o_ref[copy, 2 * tok :] = both


def pack(key_head, key_rows, value_rows, positions):
    tok = key_rows.shape[0]
    return pl.pallas_call(
        pack_kernel,
        out_shape=jax.ShapeDtypeStruct((RING, 2 * tok + 16, HD), jnp.bfloat16),
        grid_spec=pltpu.PrefetchScalarGridSpec(
            num_scalar_prefetch=1,
            grid=(1,),
            in_specs=[
                pl.BlockSpec((tok, HD), lambda i, g: (0, g[0])),
                pl.BlockSpec((tok, HD), lambda i, g: (0, g[0])),
                pl.BlockSpec((1, tok), lambda i, g: (0, 0)),
            ],
            out_specs=pl.BlockSpec((RING, 2 * tok + 16, HD), lambda i, g: (0, 0, 0)),
        ),
        name="pack",
    )(key_head, key_rows, value_rows, positions.reshape(1, tok))


def attend_kernel(q_ref, kv_ref, p_ref, o_ref):
    heads, tok, _ = q_ref.shape
    spans = kv_ref.shape[0]
    keys = jnp.concatenate([kv_ref[s, :tok, :] for s in range(spans)], axis=0)
    values = jnp.concatenate([kv_ref[s, tok : 2 * tok, :] for s in range(spans)], axis=0)
    places = []
    for s in range(spans):
        both = kv_ref[s, 2 * tok :, :].astype(jnp.float32)
        places.append(both[0:1] * 128.0 + both[1:2])
    place = jnp.concatenate(places, axis=1)
    own = p_ref[...].astype(jnp.float32)
    visible = place <= own
    for h in range(heads):
        q = q_ref[h]
        scores = lax.dot_general(
            q, keys, (((1,), (1,)), ((), ())), preferred_element_type=jnp.float32
        ) * (HD ** (-0.5))
        masked = jnp.where(visible, scores, -jnp.inf)
        top = jnp.max(masked, axis=1, keepdims=True)
        weights = jnp.exp(masked - top)
        total = jnp.sum(weights, axis=1, keepdims=True)
        mixed = jnp.dot(weights.astype(jnp.bfloat16), values, preferred_element_type=jnp.float32)
        o_ref[:, h * HD : (h + 1) * HD] = (mixed / total).astype(jnp.bfloat16)


def attend(queries, gathered, positions):
    heads, tok, _ = queries.shape
    return pl.pallas_call(
        attend_kernel,
        out_shape=jax.ShapeDtypeStruct((tok, heads * HD), jnp.bfloat16),
        compiler_params=pltpu.CompilerParams(vmem_limit_bytes=VMEM),
        name="attend",
    )(queries, gathered, positions.reshape(tok, 1))


CONTRACT = (((0,), (0,)), ((), ()))


def half_kernel(s_ref, rows_ref, own_ref, after_ref, first_ref, second_ref, before_ref, *rest):
    o_ref = rest[-1]
    me = s_ref[0]
    rows = jnp.concatenate([rows_ref[(me + d) & (RING - 1)] for d in range(RING)], axis=0)
    pieces = (own_ref, after_ref, first_ref, second_ref, before_ref)
    cols = jnp.concatenate([ref[...] for ref in pieces], axis=0)
    o_ref[...] = lax.dot_general(rows, cols, CONTRACT, preferred_element_type=jnp.float32)


def hessian_half(scalars, rows, pieces, filled=None):
    width = rows.shape[2]
    half = pieces[0].shape[1]
    whole = [pl.BlockSpec(rows.shape, lambda i, s: (0, 0, 0))]
    whole += [pl.BlockSpec(v.shape, lambda i, s: (0, 0)) for v in pieces]
    args = [scalars, rows, *pieces]
    aliases = {}
    if filled is not None:
        aliases = {len(args): 0}
        whole.append(pl.BlockSpec(memory_space=pl.ANY))
        args.append(filled)
    return pl.pallas_call(
        half_kernel,
        out_shape=jax.ShapeDtypeStruct((width, 2 * half), jnp.float32),
        grid_spec=pltpu.PrefetchScalarGridSpec(
            num_scalar_prefetch=1,
            grid=(1,),
            in_specs=whole,
            out_specs=pl.BlockSpec((width, half), lambda i, s: (0, s[1])),
        ),
        input_output_aliases=aliases,
        compiler_params=pltpu.CompilerParams(vmem_limit_bytes=VMEM),
        name="hessian_half",
    )(*args)


def shift(value, axis, by):
    return lax.ppermute(value, axis, [(i, (i + by) % RING) for i in range(RING)])


def swap_cores(value):
    return lax.ppermute(value, "core", [(0, 1), (1, 0)])


def copies(value):
    return jnp.broadcast_to(value[None], (RING,) + value.shape)


def exchange(value, axis):
    return lax.all_to_all(value, axis, split_axis=0, concat_axis=0, tiled=True)


def swap(value):
    pairs = []
    for chip in range(16):
        for core in range(2):
            for span in range(16):
                pairs.append(((chip * 2 + core) * 16 + span, (span * 2 + core) * 16 + chip))
    return lax.ppermute(value, HEAD + SEQ, pairs)


def on_device(query_rows, key_rows, value_rows, positions):
    tok = query_rows.shape[0]
    local_heads = query_rows.shape[1] // HD
    head = lax.axis_index(HEAD)
    key_head = (head * local_heads // (HEADS // KVH)).astype(jnp.int32).reshape(1)
    packed = pack(key_head, key_rows, value_rows, positions)
    gathered = exchange(packed, "x")
    queries = jnp.transpose(query_rows.reshape(tok, local_heads, HD), (1, 0, 2))
    attended = attend(queries, gathered, positions)
    chunk = swap(attended)
    rows = lax.all_gather(attended, "zh", axis=0, tiled=True)
    chunk, rows = lax.optimization_barrier((chunk, rows))
    rows = exchange(copies(rows), "x")
    own = lax.all_gather(chunk, "zl", axis=0, tiled=True)
    after, before = shift(own, "y", -1), shift(own, "y", 1)
    far_own = swap_cores(own)
    after, before, far_own = lax.optimization_barrier((after, before, far_own))
    cut = after.shape[0] // 2
    first, second, after, before = lax.optimization_barrier(
        (after[:cut], before[cut:], after, before)
    )
    first, second = shift(first, "y", -1), shift(second, "y", 1)
    far_after, far_before = swap_cores(after), swap_cores(before)
    first, second, far_after, far_before, rows = lax.optimization_barrier(
        (first, second, far_after, far_before, rows)
    )
    far_first, far_second = swap_cores(first), swap_cores(second)
    y, core = lax.axis_index("y"), lax.axis_index("core")
    near = jnp.stack([y, core]).astype(jnp.int32)
    far = jnp.stack([y, 1 - core]).astype(jnp.int32)
    hessian = hessian_half(near, rows, (own, after, first, second, before))
    far_pieces = (far_own, far_after, far_first, far_second, far_before)
    hessian = hessian_half(far, rows, far_pieces, hessian)
    return attended, hessian


def solution(mesh):
    fine = Mesh(mesh.devices.reshape(4, 4, 2, 4, 4), AXES)
    placed = (P(SEQ, HEAD), P(SEQ, None), P(SEQ, None), P(SEQ))
    return jax.shard_map(
        on_device,
        mesh=fine,
        in_specs=placed,
        out_specs=(P(SEQ, HEAD), P(HEAD, SEQ)),
        check_vma=False,
    )
```

```python
import itertools

import jax
import jax.numpy as jnp
from jax import lax
from jax.experimental import pallas as pl
from jax.experimental.pallas import tpu as pltpu
from jax.sharding import Mesh
from jax.sharding import PartitionSpec as P

HEADS = 128
KVH = 8
HD = 128
RING = 4
AXES = ("zl", "y", "core", "zh", "x")
HEAD = ("zl", "y", "core")
SEQ = ("zh", "x")
VMEM = 24 * 1024 * 1024


def pack_kernel(g_ref, k_ref, v_ref, p_ref, o_ref):
    tok = k_ref.shape[0]
    p = p_ref[...]
    high = p >> 7
    row = lax.broadcasted_iota(jnp.int32, (16, tok), 0)
    both = jnp.where(row == 0, high, p - (high << 7))
    both = both.astype(jnp.float32).astype(jnp.bfloat16)
    for copy in range(o_ref.shape[0]):
        o_ref[copy, :tok] = k_ref[...]
        o_ref[copy, tok : 2 * tok] = v_ref[...]
        o_ref[copy, 2 * tok :] = both


def pack(key_head, key_rows, value_rows, positions):
    tok = key_rows.shape[0]
    return pl.pallas_call(
        pack_kernel,
        out_shape=jax.ShapeDtypeStruct((RING, 2 * tok + 16, HD), jnp.bfloat16),
        grid_spec=pltpu.PrefetchScalarGridSpec(
            num_scalar_prefetch=1,
            grid=(1,),
            in_specs=[
                pl.BlockSpec((tok, HD), lambda i, g: (0, g[0])),
                pl.BlockSpec((tok, HD), lambda i, g: (0, g[0])),
                pl.BlockSpec((1, tok), lambda i, g: (0, 0)),
            ],
            out_specs=pl.BlockSpec((RING, 2 * tok + 16, HD), lambda i, g: (0, 0, 0)),
        ),
        name="pack",
    )(key_head, key_rows, value_rows, positions.reshape(1, tok))


def attend_kernel(q_ref, kv_ref, p_ref, o_ref):
    heads, tok, _ = q_ref.shape
    spans = kv_ref.shape[0]
    keys = jnp.concatenate([kv_ref[s, :tok, :] for s in range(spans)], axis=0)
    values = jnp.concatenate([kv_ref[s, tok : 2 * tok, :] for s in range(spans)], axis=0)
    places = []
    for s in range(spans):
        both = kv_ref[s, 2 * tok :, :].astype(jnp.float32)
        places.append(both[0:1] * 128.0 + both[1:2])
    place = jnp.concatenate(places, axis=1)
    own = p_ref[...].astype(jnp.float32)
    visible = place <= own
    for h in range(heads):
        q = q_ref[h]
        scores = lax.dot_general(
            q, keys, (((1,), (1,)), ((), ())), preferred_element_type=jnp.float32
        ) * (HD ** (-0.5))
        masked = jnp.where(visible, scores, -jnp.inf)
        top = jnp.max(masked, axis=1, keepdims=True)
        weights = jnp.exp(masked - top)
        total = jnp.sum(weights, axis=1, keepdims=True)
        mixed = jnp.dot(weights.astype(jnp.bfloat16), values, preferred_element_type=jnp.float32)
        o_ref[:, h * HD : (h + 1) * HD] = (mixed / total).astype(jnp.bfloat16)


def attend(queries, gathered, positions):
    heads, tok, _ = queries.shape
    return pl.pallas_call(
        attend_kernel,
        out_shape=jax.ShapeDtypeStruct((tok, heads * HD), jnp.bfloat16),
        compiler_params=pltpu.CompilerParams(vmem_limit_bytes=VMEM),
        name="attend",
    )(queries, gathered, positions.reshape(tok, 1))


LANDING = ((0, 2, 3, 1), (2, 1, 3, 0), (3, 0, 2, 1), (2, 0, 1, 3))
CONTRACT = (((0,), (0,)), ((), ()))


def half_kernel(s_ref, rows_ref, cols_ref, *rest):
    o_ref = rest[-1]
    x, zh = s_ref[0], s_ref[2]
    tok = cols_ref.shape[1] // RING
    blocks = []
    for d in range(RING):
        for span in range(RING):
            place = jnp.int32(LANDING[0][span])
            for group in range(1, RING):
                place = jnp.where(zh == group, LANDING[group][span], place)
            part = pl.ds(pl.multiple_of(place * tok, tok), tok)
            blocks.append(cols_ref[(x + d) & (RING - 1), part])
    cols = jnp.concatenate(blocks, axis=0)
    o_ref[...] = lax.dot_general(rows_ref[...], cols, CONTRACT, preferred_element_type=jnp.float32)


def hessian_half(scalars, rows, cols, filled=None):
    width = rows.shape[1]
    half = cols.shape[2]
    whole = [
        pl.BlockSpec(rows.shape, lambda i, s: (0, 0)),
        pl.BlockSpec(cols.shape, lambda i, s: (0, 0, 0)),
    ]
    args = [scalars, rows, cols]
    aliases = {}
    if filled is not None:
        aliases = {len(args): 0}
        whole.append(pl.BlockSpec(memory_space=pl.ANY))
        args.append(filled)
    return pl.pallas_call(
        half_kernel,
        out_shape=jax.ShapeDtypeStruct((width, 2 * half), jnp.float32),
        grid_spec=pltpu.PrefetchScalarGridSpec(
            num_scalar_prefetch=1,
            grid=(1,),
            in_specs=whole,
            out_specs=pl.BlockSpec((width, half), lambda i, s: (0, s[1])),
        ),
        input_output_aliases=aliases,
        compiler_params=pltpu.CompilerParams(vmem_limit_bytes=VMEM),
        name="hessian_half",
    )(*args)


def shift(value, axis, by):
    return lax.ppermute(value, axis, [(i, (i + by) % RING) for i in range(RING)])


def swap_cores(value):
    return lax.ppermute(value, "core", [(0, 1), (1, 0)])


def copies(value):
    return jnp.broadcast_to(value[None], (RING,) + value.shape)


def exchange(value, axis):
    return lax.all_to_all(value, axis, split_axis=0, concat_axis=0, tiled=True)


def swap(value):
    at = lambda zl, y, core, zh, x: (((zl * RING + y) * 2 + core) * RING + zh) * RING + x
    pairs = []
    for zl, y, core, zh, x in itertools.product(*(range(n) for n in (RING, RING, 2, RING, RING))):
        pairs.append((at(zl, y, core, zh, x), at(LANDING[zl][zh], x, core, zl, y)))
    return lax.ppermute(value, HEAD + SEQ, pairs)


def on_device(query_rows, key_rows, value_rows, positions):
    tok = query_rows.shape[0]
    local_heads = query_rows.shape[1] // HD
    head = lax.axis_index(HEAD)
    key_head = (head * local_heads // (HEADS // KVH)).astype(jnp.int32).reshape(1)
    packed = pack(key_head, key_rows, value_rows, positions)
    gathered = exchange(packed, "x")
    queries = jnp.transpose(query_rows.reshape(tok, local_heads, HD), (1, 0, 2))
    attended = attend(queries, gathered, positions)
    chunk = swap(attended)
    rows = lax.all_gather(attended, "zh", axis=0, tiled=True)
    chunk, rows = lax.optimization_barrier((chunk, rows))
    cols = lax.all_gather(chunk, "zl", axis=0, tiled=True)
    cols, rows = lax.optimization_barrier((cols, rows))
    near_cols = exchange(copies(cols), "y")
    after, before = shift(rows, "x", -1), shift(rows, "x", 1)
    cut = after.shape[0] // 2
    first, second = shift(after[:cut], "x", -1), shift(before[cut:], "x", 1)
    rows = jnp.concatenate([rows, after, first, second, before])
    near_cols, rows = lax.optimization_barrier((near_cols, rows))
    far_cols = swap_cores(near_cols)
    place = lax.axis_index("x"), lax.axis_index("core"), lax.axis_index("zh")
    near = jnp.stack(place).astype(jnp.int32)
    far = jnp.stack((place[0], 1 - place[1], place[2])).astype(jnp.int32)
    hessian = hessian_half(near, rows, near_cols)
    hessian = hessian_half(far, rows, far_cols, hessian)
    return attended, hessian


def solution(mesh):
    fine = Mesh(mesh.devices.reshape(4, 4, 2, 4, 4), AXES)
    placed = (P(SEQ, HEAD), P(SEQ, None), P(SEQ, None), P(SEQ))
    return jax.shard_map(
        on_device,
        mesh=fine,
        in_specs=placed,
        out_specs=(P(SEQ, HEAD), P(HEAD, SEQ)),
        check_vma=False,
    )
```

```python
import itertools

import jax
import jax.numpy as jnp
from jax import lax
from jax.experimental import pallas as pl
from jax.experimental.pallas import tpu as pltpu
from jax.sharding import Mesh
from jax.sharding import PartitionSpec as P

HEADS = 128
KVH = 8
HD = 128
RING = 4
STEPS = 2
AXES = ("zl", "y", "core", "zh", "x")
HEAD = ("zl", "y", "core")
SEQ = ("zh", "x")
VMEM = 24 * 1024 * 1024


def pack_kernel(g_ref, k_ref, v_ref, p_ref, o_ref):
    tok = k_ref.shape[0]
    p = p_ref[...]
    high = p >> 7
    row = lax.broadcasted_iota(jnp.int32, (16, tok), 0)
    both = jnp.where(row == 0, high, p - (high << 7))
    both = both.astype(jnp.float32).astype(jnp.bfloat16)
    for copy in range(o_ref.shape[0]):
        o_ref[copy, :tok] = k_ref[...]
        o_ref[copy, tok : 2 * tok] = v_ref[...]
        o_ref[copy, 2 * tok :] = both


def pack(key_head, key_rows, value_rows, positions):
    tok = key_rows.shape[0]
    return pl.pallas_call(
        pack_kernel,
        out_shape=jax.ShapeDtypeStruct((RING, 2 * tok + 16, HD), jnp.bfloat16),
        grid_spec=pltpu.PrefetchScalarGridSpec(
            num_scalar_prefetch=1,
            grid=(1,),
            in_specs=[
                pl.BlockSpec((tok, HD), lambda i, g: (0, g[0])),
                pl.BlockSpec((tok, HD), lambda i, g: (0, g[0])),
                pl.BlockSpec((1, tok), lambda i, g: (0, 0)),
            ],
            out_specs=pl.BlockSpec((RING, 2 * tok + 16, HD), lambda i, g: (0, 0, 0)),
        ),
        name="pack",
    )(key_head, key_rows, value_rows, positions.reshape(1, tok))


def attend_kernel(q_ref, kv_ref, p_ref, o_ref):
    heads, tok, _ = q_ref.shape
    spans = kv_ref.shape[0]
    keys = jnp.concatenate([kv_ref[s, :tok, :] for s in range(spans)], axis=0)
    values = jnp.concatenate([kv_ref[s, tok : 2 * tok, :] for s in range(spans)], axis=0)
    places = []
    for s in range(spans):
        both = kv_ref[s, 2 * tok :, :].astype(jnp.float32)
        places.append(both[0:1] * 128.0 + both[1:2])
    place = jnp.concatenate(places, axis=1)
    own = p_ref[...].astype(jnp.float32)
    visible = place <= own
    for h in range(heads):
        q = q_ref[h]
        scores = lax.dot_general(
            q, keys, (((1,), (1,)), ((), ())), preferred_element_type=jnp.float32
        ) * (HD ** (-0.5))
        masked = jnp.where(visible, scores, -jnp.inf)
        top = jnp.max(masked, axis=1, keepdims=True)
        weights = jnp.exp(masked - top)
        total = jnp.sum(weights, axis=1, keepdims=True)
        mixed = jnp.dot(weights.astype(jnp.bfloat16), values, preferred_element_type=jnp.float32)
        o_ref[:, h * HD : (h + 1) * HD] = (mixed / total).astype(jnp.bfloat16)


def attend(queries, gathered, positions):
    heads, tok, _ = queries.shape
    return pl.pallas_call(
        attend_kernel,
        out_shape=jax.ShapeDtypeStruct((tok, heads * HD), jnp.bfloat16),
        compiler_params=pltpu.CompilerParams(vmem_limit_bytes=VMEM),
        name="attend",
    )(queries, gathered, positions.reshape(tok, 1))


LANDING = ((0, 2, 3, 1), (2, 1, 3, 0), (3, 0, 2, 1), (2, 0, 1, 3))
CONTRACT = (((0,), (0,)), ((), ()))


def half_kernel(s_ref, rows_ref, cols_ref, *rest):
    o_ref = rest[-1]
    x, zh = s_ref[0], s_ref[2]
    tok = cols_ref.shape[1] // RING
    blocks = []
    for d in range(RING):
        for span in range(RING):
            place = jnp.int32(LANDING[0][span])
            for group in range(1, RING):
                place = jnp.where(zh == group, LANDING[group][span], place)
            part = pl.ds(pl.multiple_of(place * tok, tok), tok)
            blocks.append(cols_ref[(x + d) & (RING - 1), part])
    cols = jnp.concatenate(blocks, axis=0)
    o_ref[...] = lax.dot_general(rows_ref[...], cols, CONTRACT, preferred_element_type=jnp.float32)


def hessian_half(scalars, rows, cols, filled=None):
    width = rows.shape[1]
    half = cols.shape[2]
    whole = [
        pl.BlockSpec(rows.shape, lambda i, s: (0, 0)),
        pl.BlockSpec((*cols.shape[:2], half // STEPS), lambda i, s: (0, 0, i)),
    ]
    args = [scalars, rows, cols]
    aliases = {}
    if filled is not None:
        aliases = {len(args): 0}
        whole.append(pl.BlockSpec(memory_space=pl.ANY))
        args.append(filled)
    return pl.pallas_call(
        half_kernel,
        out_shape=jax.ShapeDtypeStruct((width, 2 * half), jnp.float32),
        grid_spec=pltpu.PrefetchScalarGridSpec(
            num_scalar_prefetch=1,
            grid=(STEPS,),
            in_specs=whole,
            out_specs=pl.BlockSpec((width, half // STEPS), lambda i, s: (0, s[1] * STEPS + i)),
        ),
        input_output_aliases=aliases,
        compiler_params=pltpu.CompilerParams(vmem_limit_bytes=VMEM),
        name="hessian_half",
    )(*args)


def shift(value, axis, by):
    return lax.ppermute(value, axis, [(i, (i + by) % RING) for i in range(RING)])


def swap_cores(value):
    return lax.ppermute(value, "core", [(0, 1), (1, 0)])


def copies(value):
    return jnp.broadcast_to(value[None], (RING,) + value.shape)


def exchange(value, axis):
    return lax.all_to_all(value, axis, split_axis=0, concat_axis=0, tiled=True)


def swap(value):
    at = lambda zl, y, core, zh, x: (((zl * RING + y) * 2 + core) * RING + zh) * RING + x
    pairs = []
    for zl, y, core, zh, x in itertools.product(*(range(n) for n in (RING, RING, 2, RING, RING))):
        pairs.append((at(zl, y, core, zh, x), at(LANDING[zl][zh], x, core, zl, y)))
    return lax.ppermute(value, HEAD + SEQ, pairs)


def on_device(query_rows, key_rows, value_rows, positions):
    tok = query_rows.shape[0]
    local_heads = query_rows.shape[1] // HD
    head = lax.axis_index(HEAD)
    key_head = (head * local_heads // (HEADS // KVH)).astype(jnp.int32).reshape(1)
    packed = pack(key_head, key_rows, value_rows, positions)
    gathered = exchange(packed, "x")
    queries = jnp.transpose(query_rows.reshape(tok, local_heads, HD), (1, 0, 2))
    attended = attend(queries, gathered, positions)
    chunk = swap(attended)
    rows = lax.all_gather(attended, "zh", axis=0, tiled=True)
    chunk, rows = lax.optimization_barrier((chunk, rows))
    cols = lax.all_gather(chunk, "zl", axis=0, tiled=True)
    after, before = shift(rows, "x", -1), shift(rows, "x", 1)
    cols, after, before = lax.optimization_barrier((cols, after, before))
    near_cols = exchange(copies(cols), "y")
    cut = after.shape[0] // 2
    first, second = shift(after[:cut], "x", -1), shift(before[cut:], "x", 1)
    rows = jnp.concatenate([rows, after, first, second, before])
    near_cols, rows = lax.optimization_barrier((near_cols, rows))
    far_cols = swap_cores(near_cols)
    place = lax.axis_index("x"), lax.axis_index("core"), lax.axis_index("zh")
    near = jnp.stack(place).astype(jnp.int32)
    far = jnp.stack((place[0], 1 - place[1], place[2])).astype(jnp.int32)
    hessian = hessian_half(near, rows, near_cols)
    hessian = hessian_half(far, rows, far_cols, hessian)
    return attended, hessian


def solution(mesh):
    fine = Mesh(mesh.devices.reshape(4, 4, 2, 4, 4), AXES)
    placed = (P(SEQ, HEAD), P(SEQ, None), P(SEQ, None), P(SEQ))
    return jax.shard_map(
        on_device,
        mesh=fine,
        in_specs=placed,
        out_specs=(P(SEQ, HEAD), P(HEAD, SEQ)),
        check_vma=False,
    )
```

```python
import itertools

import jax
import jax.numpy as jnp
from jax import lax
from jax.experimental import pallas as pl
from jax.experimental.pallas import tpu as pltpu
from jax.sharding import Mesh
from jax.sharding import PartitionSpec as P

HEADS = 128
KVH = 8
HD = 128
RING = 4
STEPS = 2
AXES = ("zl", "y", "core", "zh", "x")
HEAD = ("zl", "y", "core")
SEQ = ("zh", "x")
VMEM = 24 * 1024 * 1024


def pack_kernel(g_ref, k_ref, v_ref, p_ref, o_ref):
    tok = k_ref.shape[0]
    p = p_ref[...]
    high = p >> 7
    row = lax.broadcasted_iota(jnp.int32, (16, tok), 0)
    both = jnp.where(row == 0, high, p - (high << 7))
    both = both.astype(jnp.float32).astype(jnp.bfloat16)
    for copy in range(o_ref.shape[0]):
        o_ref[copy, :tok] = k_ref[...]
        o_ref[copy, tok : 2 * tok] = v_ref[...]
        o_ref[copy, 2 * tok :] = both


def pack(key_head, key_rows, value_rows, positions):
    tok = key_rows.shape[0]
    return pl.pallas_call(
        pack_kernel,
        out_shape=jax.ShapeDtypeStruct((RING, 2 * tok + 16, HD), jnp.bfloat16),
        grid_spec=pltpu.PrefetchScalarGridSpec(
            num_scalar_prefetch=1,
            grid=(1,),
            in_specs=[
                pl.BlockSpec((tok, HD), lambda i, g: (0, g[0])),
                pl.BlockSpec((tok, HD), lambda i, g: (0, g[0])),
                pl.BlockSpec((1, tok), lambda i, g: (0, 0)),
            ],
            out_specs=pl.BlockSpec((RING, 2 * tok + 16, HD), lambda i, g: (0, 0, 0)),
        ),
        name="pack",
    )(key_head, key_rows, value_rows, positions.reshape(1, tok))


def attend_kernel(q_ref, kv_ref, p_ref, o_ref):
    heads, tok, _ = q_ref.shape
    spans = kv_ref.shape[0]
    keys = jnp.concatenate([kv_ref[s, :tok, :] for s in range(spans)], axis=0)
    values = jnp.concatenate([kv_ref[s, tok : 2 * tok, :] for s in range(spans)], axis=0)
    places = []
    for s in range(spans):
        both = kv_ref[s, 2 * tok :, :].astype(jnp.float32)
        places.append(both[0:1] * 128.0 + both[1:2])
    place = jnp.concatenate(places, axis=1)
    own = p_ref[...].astype(jnp.float32)
    visible = place <= own
    for h in range(heads):
        q = q_ref[h]
        scores = lax.dot_general(
            q, keys, (((1,), (1,)), ((), ())), preferred_element_type=jnp.float32
        ) * (HD ** (-0.5))
        masked = jnp.where(visible, scores, -jnp.inf)
        top = jnp.max(masked, axis=1, keepdims=True)
        weights = jnp.exp(masked - top)
        total = jnp.sum(weights, axis=1, keepdims=True)
        mixed = jnp.dot(weights.astype(jnp.bfloat16), values, preferred_element_type=jnp.float32)
        o_ref[:, h * HD : (h + 1) * HD] = (mixed / total).astype(jnp.bfloat16)


def attend(queries, gathered, positions):
    heads, tok, _ = queries.shape
    return pl.pallas_call(
        attend_kernel,
        out_shape=jax.ShapeDtypeStruct((tok, heads * HD), jnp.bfloat16),
        compiler_params=pltpu.CompilerParams(vmem_limit_bytes=VMEM),
        name="attend",
    )(queries, gathered, positions.reshape(tok, 1))


LANDING = ((0, 2, 3, 1), (2, 1, 3, 0), (3, 0, 2, 1), (2, 0, 1, 3))
TAKEN = tuple(tuple(line.index(k) for k in range(RING)) for line in LANDING)
CONTRACT = (((0,), (0,)), ((), ()))


def ordered_kernel(s_ref, v_ref, o_ref):
    for copy in range(RING):
        o_ref[copy] = v_ref[...]


def ordered_copies(order, value):
    depth, width = value.shape
    part = depth // RING
    return pl.pallas_call(
        ordered_kernel,
        out_shape=jax.ShapeDtypeStruct((RING, depth, width), value.dtype),
        grid_spec=pltpu.PrefetchScalarGridSpec(
            num_scalar_prefetch=1,
            grid=(RING,),
            in_specs=[pl.BlockSpec((part, width), lambda i, s: (s[i], 0))],
            out_specs=pl.BlockSpec((RING, part, width), lambda i, s: (0, i, 0)),
        ),
        name="ordered_copies",
    )(order, value)


def hessian_kernel(s_ref, rows_ref, near_ref, far_ref, o_ref):
    step = pl.program_id(0)

    def product(cols_ref):
        cols = cols_ref[...].reshape(rows_ref.shape[0], cols_ref.shape[2])
        o_ref[...] = lax.dot_general(
            rows_ref[...], cols, CONTRACT, preferred_element_type=jnp.float32
        )

    @pl.when(step < STEPS)
    def _():
        product(near_ref)

    @pl.when(step >= STEPS)
    def _():
        product(far_ref)


def hessian_of(core, rows, near, far):
    depth, width = rows.shape
    ring, part, half = near.shape
    block = (ring, part, half // STEPS)
    return pl.pallas_call(
        hessian_kernel,
        out_shape=jax.ShapeDtypeStruct((width, 2 * half), jnp.float32),
        grid_spec=pltpu.PrefetchScalarGridSpec(
            num_scalar_prefetch=1,
            grid=(2 * STEPS,),
            in_specs=[
                pl.BlockSpec((depth, width), lambda i, s: (0, 0)),
                pl.BlockSpec(block, lambda i, s: (0, 0, jnp.minimum(i, STEPS - 1))),
                pl.BlockSpec(block, lambda i, s: (0, 0, jnp.maximum(i - STEPS, 0))),
            ],
            out_specs=pl.BlockSpec(
                (width, half // STEPS), lambda i, s: (0, (i + s[0] * STEPS) % (2 * STEPS))
            ),
        ),
        compiler_params=pltpu.CompilerParams(vmem_limit_bytes=VMEM),
        name="hessian",
    )(core, rows, near, far)


def swap_cores(value):
    return lax.ppermute(value, "core", [(0, 1), (1, 0)])


def copies(value):
    return jnp.broadcast_to(value[None], (RING,) + value.shape)


def exchange(value, axis):
    return lax.all_to_all(value, axis, split_axis=0, concat_axis=0, tiled=True)


def swap(value):
    at = lambda zl, y, core, zh, x: (((zl * RING + y) * 2 + core) * RING + zh) * RING + x
    pairs = []
    for zl, y, core, zh, x in itertools.product(*(range(n) for n in (RING, RING, 2, RING, RING))):
        pairs.append((at(zl, y, core, zh, x), at(LANDING[zl][zh], x, core, zl, y)))
    return lax.ppermute(value, HEAD + SEQ, pairs)


def on_device(query_rows, key_rows, value_rows, positions):
    tok = query_rows.shape[0]
    local_heads = query_rows.shape[1] // HD
    head = lax.axis_index(HEAD)
    key_head = (head * local_heads // (HEADS // KVH)).astype(jnp.int32).reshape(1)
    packed = pack(key_head, key_rows, value_rows, positions)
    gathered = exchange(packed, "x")
    queries = jnp.transpose(query_rows.reshape(tok, local_heads, HD), (1, 0, 2))
    attended = attend(queries, gathered, positions)
    chunk = swap(attended)
    cols = lax.all_gather(chunk, "zl", axis=0, tiled=True)
    cols, mine = lax.optimization_barrier((cols, attended))
    near = exchange(copies(cols), "y")
    rows = lax.all_gather(mine, "zh", axis=0, tiled=True)
    order = jnp.asarray(TAKEN, jnp.int32)[lax.axis_index("zh")]
    near, rows = lax.optimization_barrier((near, ordered_copies(order, rows)))
    rows = exchange(rows, "x")
    far = swap_cores(near)
    core = lax.axis_index("core").astype(jnp.int32).reshape(1)
    hessian = hessian_of(core, rows.reshape(-1, rows.shape[2]), near, far)
    return attended, hessian


def solution(mesh):
    fine = Mesh(mesh.devices.reshape(4, 4, 2, 4, 4), AXES)
    placed = (P(SEQ, HEAD), P(SEQ, None), P(SEQ, None), P(SEQ))
    return jax.shard_map(
        on_device,
        mesh=fine,
        in_specs=placed,
        out_specs=(P(SEQ, HEAD), P(HEAD, SEQ)),
        check_vma=False,
    )
```

```python
import itertools

import jax
import jax.numpy as jnp
from jax import lax
from jax.experimental import pallas as pl
from jax.experimental.pallas import tpu as pltpu
from jax.sharding import Mesh
from jax.sharding import PartitionSpec as P

HEADS = 128
KVH = 8
HD = 128
RING = 4
STEPS = 2
AXES = ("zl", "y", "core", "zh", "x")
HEAD = ("zl", "y", "core")
SEQ = ("zh", "x")
VMEM = 24 * 1024 * 1024


def pack_kernel(g_ref, k_ref, v_ref, p_ref, o_ref):
    tok = k_ref.shape[0]
    p = p_ref[...]
    high = p >> 7
    row = lax.broadcasted_iota(jnp.int32, (16, tok), 0)
    both = jnp.where(row == 0, high, p - (high << 7))
    both = both.astype(jnp.float32).astype(jnp.bfloat16)
    for copy in range(o_ref.shape[0]):
        o_ref[copy, :tok] = k_ref[...]
        o_ref[copy, tok : 2 * tok] = v_ref[...]
        o_ref[copy, 2 * tok :] = both


def pack(key_head, key_rows, value_rows, positions):
    tok = key_rows.shape[0]
    return pl.pallas_call(
        pack_kernel,
        out_shape=jax.ShapeDtypeStruct((RING, 2 * tok + 16, HD), jnp.bfloat16),
        grid_spec=pltpu.PrefetchScalarGridSpec(
            num_scalar_prefetch=1,
            grid=(1,),
            in_specs=[
                pl.BlockSpec((tok, HD), lambda i, g: (0, g[0])),
                pl.BlockSpec((tok, HD), lambda i, g: (0, g[0])),
                pl.BlockSpec((1, tok), lambda i, g: (0, 0)),
            ],
            out_specs=pl.BlockSpec((RING, 2 * tok + 16, HD), lambda i, g: (0, 0, 0)),
        ),
        name="pack",
    )(key_head, key_rows, value_rows, positions.reshape(1, tok))


def attend_kernel(q_ref, kv_ref, p_ref, o_ref):
    heads, tok, _ = q_ref.shape
    spans = kv_ref.shape[0]
    keys = jnp.concatenate([kv_ref[s, :tok, :] for s in range(spans)], axis=0)
    values = jnp.concatenate([kv_ref[s, tok : 2 * tok, :] for s in range(spans)], axis=0)
    places = []
    for s in range(spans):
        both = kv_ref[s, 2 * tok :, :].astype(jnp.float32)
        places.append(both[0:1] * 128.0 + both[1:2])
    place = jnp.concatenate(places, axis=1)
    own = p_ref[...].astype(jnp.float32)
    visible = place <= own
    for h in range(heads):
        q = q_ref[h]
        scores = lax.dot_general(
            q, keys, (((1,), (1,)), ((), ())), preferred_element_type=jnp.float32
        ) * (HD ** (-0.5))
        masked = jnp.where(visible, scores, -jnp.inf)
        top = jnp.max(masked, axis=1, keepdims=True)
        weights = jnp.exp(masked - top)
        total = jnp.sum(weights, axis=1, keepdims=True)
        mixed = jnp.dot(weights.astype(jnp.bfloat16), values, preferred_element_type=jnp.float32)
        o_ref[:, h * HD : (h + 1) * HD] = (mixed / total).astype(jnp.bfloat16)


def attend(queries, gathered, positions):
    heads, tok, _ = queries.shape
    return pl.pallas_call(
        attend_kernel,
        out_shape=jax.ShapeDtypeStruct((tok, heads * HD), jnp.bfloat16),
        compiler_params=pltpu.CompilerParams(vmem_limit_bytes=VMEM),
        name="attend",
    )(queries, gathered, positions.reshape(tok, 1))


LANDING = ((0, 2, 3, 1), (1, 3, 2, 0), (3, 1, 0, 2), (2, 0, 1, 3))
CONTRACT = (((0,), (0,)), ((), ()))


def half_kernel(s_ref, rows_ref, cols_ref, *rest):
    o_ref = rest[-1]
    o_ref[...] = lax.dot_general(
        rows_ref[...], cols_ref[...], CONTRACT, preferred_element_type=jnp.float32
    )


def hessian_half(place, rows, cols, filled=None):
    depth, width = rows.shape
    half = cols.shape[1]
    specs = [
        pl.BlockSpec((depth, width), lambda i, s: (0, 0)),
        pl.BlockSpec((depth, half // STEPS), lambda i, s: (0, i)),
    ]
    args = [place, rows, cols]
    aliases = {}
    if filled is not None:
        aliases = {len(args): 0}
        specs.append(pl.BlockSpec(memory_space=pl.ANY))
        args.append(filled)
    return pl.pallas_call(
        half_kernel,
        out_shape=jax.ShapeDtypeStruct((width, 2 * half), jnp.float32),
        grid_spec=pltpu.PrefetchScalarGridSpec(
            num_scalar_prefetch=1,
            grid=(STEPS,),
            in_specs=specs,
            out_specs=pl.BlockSpec((width, half // STEPS), lambda i, s: (0, s[0] * STEPS + i)),
        ),
        input_output_aliases=aliases,
        compiler_params=pltpu.CompilerParams(vmem_limit_bytes=VMEM),
        name="hessian_half",
    )(*args)


def turn(value, axis, by):
    at = lambda core, i: core * RING + i if axis == "x" else i * 2 + core
    axes = ("core", axis) if axis == "x" else (axis, "core")
    steps = ((0, by), (1, -by))
    pairs = [(at(c, i), at(c, (i + d) % RING)) for c, d in steps for i in range(RING)]
    return lax.ppermute(value, axes, pairs)


def joined(axis, own, got, across):
    me = lax.axis_index(axis)
    ahead = jnp.where(lax.axis_index("core") == 0, RING - 1, 1)
    depth, width = own.shape
    slots = (me, me + ahead, me - ahead, me + 2, me + 2)
    whole = jnp.zeros((RING * depth, width), own.dtype)
    for slot, piece, shift in zip(slots, (own, *got, *across), (0, 0, 0, 0, depth // 2)):
        start = (slot & (RING - 1)) * depth + shift
        whole = lax.dynamic_update_slice(whole, piece, (start, 0))
    return whole


def swap_cores(value):
    return lax.ppermute(value, "core", [(0, 1), (1, 0)])


def exchange(value, axis):
    return lax.all_to_all(value, axis, split_axis=0, concat_axis=0, tiled=True)


def swap(value):
    at = lambda zl, y, core, zh, x: (((zl * RING + y) * 2 + core) * RING + zh) * RING + x
    pairs = []
    for zl, y, core, zh, x in itertools.product(*(range(n) for n in (RING, RING, 2, RING, RING))):
        pairs.append((at(zl, y, core, zh, x), at(LANDING[zl][zh], x, core, zl, y)))
    return lax.ppermute(value, HEAD + SEQ, pairs)


def on_device(query_rows, key_rows, value_rows, positions):
    tok = query_rows.shape[0]
    local_heads = query_rows.shape[1] // HD
    head = lax.axis_index(HEAD)
    key_head = (head * local_heads // (HEADS // KVH)).astype(jnp.int32).reshape(1)
    packed = pack(key_head, key_rows, value_rows, positions)
    gathered = exchange(packed, "x")
    queries = jnp.transpose(query_rows.reshape(tok, local_heads, HD), (1, 0, 2))
    attended = attend(queries, gathered, positions)
    chunk = swap(attended)
    rows = lax.all_gather(attended, "zh", axis=0, tiled=True)
    chunk, rows = lax.optimization_barrier((chunk, rows))
    landed = [[place * RING + group for place in LANDING[group]] for group in range(RING)]
    cols = lax.all_gather(chunk, ("zl", "zh"), axis=0, tiled=True, axis_index_groups=landed)
    cols, rows = lax.optimization_barrier((cols, rows))
    ways = ((rows, "x"), (cols, "y"))
    got = [[turn(v, axis, by) for v, axis in ways] for by in (1, -1)]
    half = rows.shape[0] // 2
    cut = lax.optimization_barrier([[v[:half] for v in got[0]], [v[half:] for v in got[1]]])
    across = [[turn(v, "xy"[k], by) for k, v in enumerate(c)] for c, by in zip(cut, (1, -1))]
    rows, near = (
        joined("xy"[k], v, (got[0][k], got[1][k]), (across[0][k], across[1][k]))
        for k, v in enumerate((rows, cols))
    )
    near, rows = lax.optimization_barrier((near, rows))
    far = swap_cores(near)
    core = lax.axis_index("core").astype(jnp.int32).reshape(1)
    hessian = hessian_half(core, rows, near)
    hessian = hessian_half(1 - core, rows, far, hessian)
    return attended, hessian


def solution(mesh):
    fine = Mesh(mesh.devices.reshape(4, 4, 2, 4, 4), AXES)
    placed = (P(SEQ, HEAD), P(SEQ, None), P(SEQ, None), P(SEQ))
    return jax.shard_map(
        on_device,
        mesh=fine,
        in_specs=placed,
        out_specs=(P(SEQ, HEAD), P(HEAD, SEQ)),
        check_vma=False,
    )
```

```python
import itertools

import jax
import jax.numpy as jnp
from jax import lax
from jax.experimental import pallas as pl
from jax.experimental.pallas import tpu as pltpu
from jax.sharding import Mesh
from jax.sharding import PartitionSpec as P

HEADS = 128
KVH = 8
HD = 128
RING = 4
STEPS = 2
AXES = ("zl", "y", "core", "zh", "x")
HEAD = ("zl", "y", "core")
SEQ = ("zh", "x")
VMEM = 24 * 1024 * 1024


def pack_kernel(g_ref, k_ref, v_ref, p_ref, o_ref):
    tok = k_ref.shape[0]
    p = p_ref[...]
    high = p >> 7
    row = lax.broadcasted_iota(jnp.int32, (16, tok), 0)
    both = jnp.where(row == 0, high, p - (high << 7))
    both = both.astype(jnp.float32).astype(jnp.bfloat16)
    for copy in range(o_ref.shape[0]):
        o_ref[copy, :tok] = k_ref[...]
        o_ref[copy, tok : 2 * tok] = v_ref[...]
        o_ref[copy, 2 * tok :] = both


def pack(key_head, key_rows, value_rows, positions):
    tok = key_rows.shape[0]
    return pl.pallas_call(
        pack_kernel,
        out_shape=jax.ShapeDtypeStruct((RING, 2 * tok + 16, HD), jnp.bfloat16),
        grid_spec=pltpu.PrefetchScalarGridSpec(
            num_scalar_prefetch=1,
            grid=(1,),
            in_specs=[
                pl.BlockSpec((tok, HD), lambda i, g: (0, g[0])),
                pl.BlockSpec((tok, HD), lambda i, g: (0, g[0])),
                pl.BlockSpec((1, tok), lambda i, g: (0, 0)),
            ],
            out_specs=pl.BlockSpec((RING, 2 * tok + 16, HD), lambda i, g: (0, 0, 0)),
        ),
        name="pack",
    )(key_head, key_rows, value_rows, positions.reshape(1, tok))


def attend_kernel(q_ref, kv_ref, p_ref, o_ref):
    heads, tok, _ = q_ref.shape
    spans = kv_ref.shape[0]
    keys = jnp.concatenate([kv_ref[s, :tok, :] for s in range(spans)], axis=0)
    values = jnp.concatenate([kv_ref[s, tok : 2 * tok, :] for s in range(spans)], axis=0)
    places = []
    for s in range(spans):
        both = kv_ref[s, 2 * tok :, :].astype(jnp.float32)
        places.append(both[0:1] * 128.0 + both[1:2])
    place = jnp.concatenate(places, axis=1)
    own = p_ref[...].astype(jnp.float32)
    visible = place <= own
    for h in range(heads):
        q = q_ref[h]
        scores = lax.dot_general(
            q, keys, (((1,), (1,)), ((), ())), preferred_element_type=jnp.float32
        ) * (HD ** (-0.5))
        masked = jnp.where(visible, scores, -jnp.inf)
        top = jnp.max(masked, axis=1, keepdims=True)
        weights = jnp.exp(masked - top)
        total = jnp.sum(weights, axis=1, keepdims=True)
        mixed = jnp.dot(weights.astype(jnp.bfloat16), values, preferred_element_type=jnp.float32)
        o_ref[:, h * HD : (h + 1) * HD] = (mixed / total).astype(jnp.bfloat16)


def attend(queries, gathered, positions):
    heads, tok, _ = queries.shape
    return pl.pallas_call(
        attend_kernel,
        out_shape=jax.ShapeDtypeStruct((tok, heads * HD), jnp.bfloat16),
        compiler_params=pltpu.CompilerParams(vmem_limit_bytes=VMEM),
        name="attend",
    )(queries, gathered, positions.reshape(tok, 1))


LANDING = ((0, 2, 3, 1), (1, 3, 2, 0), (3, 1, 0, 2), (2, 0, 1, 3))
CONTRACT = (((0,), (0,)), ((), ()))


def hessian_kernel(s_ref, rows_ref, near_ref, far_ref, o_ref):
    step = pl.program_id(0)

    def product(cols_ref):
        cols = cols_ref[...].reshape(rows_ref.shape[0], cols_ref.shape[2])
        o_ref[...] = lax.dot_general(
            rows_ref[...], cols, CONTRACT, preferred_element_type=jnp.float32
        )

    @pl.when(step < STEPS)
    def _():
        product(near_ref)

    @pl.when(step >= STEPS)
    def _():
        product(far_ref)


def hessian_of(core, rows, near, far):
    depth, width = rows.shape
    ring, part, half = near.shape
    block = (ring, part, half // STEPS)
    return pl.pallas_call(
        hessian_kernel,
        out_shape=jax.ShapeDtypeStruct((width, 2 * half), jnp.float32),
        grid_spec=pltpu.PrefetchScalarGridSpec(
            num_scalar_prefetch=1,
            grid=(2 * STEPS,),
            in_specs=[
                pl.BlockSpec((depth, width), lambda i, s: (0, 0)),
                pl.BlockSpec(block, lambda i, s: (0, 0, jnp.minimum(i, STEPS - 1))),
                pl.BlockSpec(block, lambda i, s: (0, 0, jnp.maximum(i - STEPS, 0))),
            ],
            out_specs=pl.BlockSpec(
                (width, half // STEPS), lambda i, s: (0, (i + s[0] * STEPS) % (2 * STEPS))
            ),
        ),
        compiler_params=pltpu.CompilerParams(vmem_limit_bytes=VMEM),
        name="hessian",
    )(core, rows, near, far)


def shift(value, axis, by):
    return lax.ppermute(value, axis, [(i, (i + by) % RING) for i in range(RING)])


def joined(axis, own, after, before, across):
    me = lax.axis_index(axis)
    depth, width = own.shape
    pieces = ((own, 0, 0), (after, 1, 0), (before, 3, 0), (across[0], 2, 0), (across[1], 2, depth // 2))
    whole = jnp.zeros((RING * depth, width), own.dtype)
    for piece, ahead, more in pieces:
        start = ((me + ahead) & (RING - 1)) * depth + more
        whole = lax.dynamic_update_slice(whole, piece, (start, 0))
    return whole


def copies(value):
    return jnp.broadcast_to(value[None], (RING,) + value.shape)


def swap_cores(value):
    return lax.ppermute(value, "core", [(0, 1), (1, 0)])


def exchange(value, axis):
    return lax.all_to_all(value, axis, split_axis=0, concat_axis=0, tiled=True)


def swap(value):
    at = lambda zl, y, core, zh, x: (((zl * RING + y) * 2 + core) * RING + zh) * RING + x
    pairs = []
    for zl, y, core, zh, x in itertools.product(*(range(n) for n in (RING, RING, 2, RING, RING))):
        pairs.append((at(zl, y, core, zh, x), at(LANDING[zl][zh], x, core, zl, y)))
    return lax.ppermute(value, HEAD + SEQ, pairs)


def on_device(query_rows, key_rows, value_rows, positions):
    tok = query_rows.shape[0]
    local_heads = query_rows.shape[1] // HD
    head = lax.axis_index(HEAD)
    key_head = (head * local_heads // (HEADS // KVH)).astype(jnp.int32).reshape(1)
    packed = pack(key_head, key_rows, value_rows, positions)
    gathered = exchange(packed, "x")
    queries = jnp.transpose(query_rows.reshape(tok, local_heads, HD), (1, 0, 2))
    attended = attend(queries, gathered, positions)
    chunk = swap(attended)
    rows = lax.all_gather(attended, "zh", axis=0, tiled=True)
    chunk, rows = lax.optimization_barrier((chunk, rows))
    landed = [[place * RING + group for place in LANDING[group]] for group in range(RING)]
    cols = lax.all_gather(chunk, ("zl", "zh"), axis=0, tiled=True, axis_index_groups=landed)
    cols, rows = lax.optimization_barrier((cols, rows))
    near = exchange(copies(cols), "y")
    after, before = shift(rows, "x", -1), shift(rows, "x", 1)
    cut = after.shape[0] // 2
    across = shift(after[:cut], "x", -1), shift(before[cut:], "x", 1)
    near, _, _ = lax.optimization_barrier((near, after, before))
    far = swap_cores(near)
    across, far = lax.optimization_barrier((across, far))
    rows = joined("x", rows, after, before, across)
    core = lax.axis_index("core").astype(jnp.int32).reshape(1)
    hessian = hessian_of(core, rows, near, far)
    return attended, hessian


def solution(mesh):
    fine = Mesh(mesh.devices.reshape(4, 4, 2, 4, 4), AXES)
    placed = (P(SEQ, HEAD), P(SEQ, None), P(SEQ, None), P(SEQ))
    return jax.shard_map(
        on_device,
        mesh=fine,
        in_specs=placed,
        out_specs=(P(SEQ, HEAD), P(HEAD, SEQ)),
        check_vma=False,
    )
```

```python
import itertools

import jax
import jax.numpy as jnp
from jax import lax
from jax.experimental import pallas as pl
from jax.experimental.pallas import tpu as pltpu
from jax.sharding import Mesh
from jax.sharding import PartitionSpec as P

HEADS = 128
KVH = 8
HD = 128
RING = 4
STEPS = 2
AXES = ("zl", "y", "core", "zh", "x")
HEAD = ("zl", "y", "core")
SEQ = ("zh", "x")
VMEM = 24 * 1024 * 1024


def pack_kernel(g_ref, k_ref, v_ref, p_ref, o_ref):
    tok = k_ref.shape[0]
    p = p_ref[...]
    high = p >> 7
    row = lax.broadcasted_iota(jnp.int32, (16, tok), 0)
    both = jnp.where(row == 0, high, p - (high << 7))
    both = both.astype(jnp.float32).astype(jnp.bfloat16)
    for copy in range(o_ref.shape[0]):
        o_ref[copy, :tok] = k_ref[...]
        o_ref[copy, tok : 2 * tok] = v_ref[...]
        o_ref[copy, 2 * tok :] = both


def pack(key_head, key_rows, value_rows, positions):
    tok = key_rows.shape[0]
    return pl.pallas_call(
        pack_kernel,
        out_shape=jax.ShapeDtypeStruct((RING, 2 * tok + 16, HD), jnp.bfloat16),
        grid_spec=pltpu.PrefetchScalarGridSpec(
            num_scalar_prefetch=1,
            grid=(1,),
            in_specs=[
                pl.BlockSpec((tok, HD), lambda i, g: (0, g[0])),
                pl.BlockSpec((tok, HD), lambda i, g: (0, g[0])),
                pl.BlockSpec((1, tok), lambda i, g: (0, 0)),
            ],
            out_specs=pl.BlockSpec((RING, 2 * tok + 16, HD), lambda i, g: (0, 0, 0)),
        ),
        name="pack",
    )(key_head, key_rows, value_rows, positions.reshape(1, tok))


def attend_kernel(q_ref, kv_ref, p_ref, o_ref):
    heads, tok, _ = q_ref.shape
    spans = kv_ref.shape[0]
    keys = jnp.concatenate([kv_ref[s, :tok, :] for s in range(spans)], axis=0)
    values = jnp.concatenate([kv_ref[s, tok : 2 * tok, :] for s in range(spans)], axis=0)
    places = []
    for s in range(spans):
        both = kv_ref[s, 2 * tok :, :].astype(jnp.float32)
        places.append(both[0:1] * 128.0 + both[1:2])
    place = jnp.concatenate(places, axis=1)
    own = p_ref[...].astype(jnp.float32)
    visible = place <= own
    for h in range(heads):
        q = q_ref[h]
        scores = lax.dot_general(
            q, keys, (((1,), (1,)), ((), ())), preferred_element_type=jnp.float32
        ) * (HD ** (-0.5))
        masked = jnp.where(visible, scores, -jnp.inf)
        top = jnp.max(masked, axis=1, keepdims=True)
        weights = jnp.exp(masked - top)
        total = jnp.sum(weights, axis=1, keepdims=True)
        mixed = jnp.dot(weights.astype(jnp.bfloat16), values, preferred_element_type=jnp.float32)
        o_ref[:, h * HD : (h + 1) * HD] = (mixed / total).astype(jnp.bfloat16)


def attend(queries, gathered, positions):
    heads, tok, _ = queries.shape
    return pl.pallas_call(
        attend_kernel,
        out_shape=jax.ShapeDtypeStruct((tok, heads * HD), jnp.bfloat16),
        compiler_params=pltpu.CompilerParams(vmem_limit_bytes=VMEM),
        name="attend",
    )(queries, gathered, positions.reshape(tok, 1))


LANDING = ((0, 2, 3, 1), (1, 3, 2, 0), (3, 1, 0, 2), (2, 0, 1, 3))
CONTRACT = (((0,), (0,)), ((), ()))


def half_kernel(s_ref, rows_ref, cols_ref, *rest):
    o_ref = rest[-1]
    o_ref[...] = lax.dot_general(
        rows_ref[...], cols_ref[...], CONTRACT, preferred_element_type=jnp.float32
    )


def hessian_half(place, rows, cols, filled=None):
    depth, width = rows.shape
    half = cols.shape[1]
    specs = [
        pl.BlockSpec((depth, width), lambda i, s: (0, 0)),
        pl.BlockSpec((depth, half // STEPS), lambda i, s: (0, i)),
    ]
    args = [place, rows, cols]
    aliases = {}
    if filled is not None:
        aliases = {len(args): 0}
        specs.append(pl.BlockSpec(memory_space=pl.ANY))
        args.append(filled)
    return pl.pallas_call(
        half_kernel,
        out_shape=jax.ShapeDtypeStruct((width, 2 * half), jnp.float32),
        grid_spec=pltpu.PrefetchScalarGridSpec(
            num_scalar_prefetch=1,
            grid=(STEPS,),
            in_specs=specs,
            out_specs=pl.BlockSpec((width, half // STEPS), lambda i, s: (0, s[0] * STEPS + i)),
        ),
        input_output_aliases=aliases,
        compiler_params=pltpu.CompilerParams(vmem_limit_bytes=VMEM),
        name="hessian_half",
    )(*args)


def shift(value, axis, by):
    return lax.ppermute(value, axis, [(i, (i + by) % RING) for i in range(RING)])


def joined(axis, pieces):
    me = lax.axis_index(axis)
    depth, width = pieces[0].shape
    whole = jnp.zeros((RING * depth, width), pieces[0].dtype)
    for ahead, piece in enumerate(pieces):
        start = ((me + ahead) & (RING - 1)) * depth
        whole = lax.dynamic_update_slice(whole, piece, (start, 0))
    return whole


def copies(value):
    return jnp.broadcast_to(value[None], (RING,) + value.shape)


def swap_cores(value):
    return lax.ppermute(value, "core", [(0, 1), (1, 0)])


def exchange(value, axis):
    return lax.all_to_all(value, axis, split_axis=0, concat_axis=0, tiled=True)


def swap(value):
    at = lambda zl, y, core, zh, x: (((zl * RING + y) * 2 + core) * RING + zh) * RING + x
    pairs = []
    for zl, y, core, zh, x in itertools.product(*(range(n) for n in (RING, RING, 2, RING, RING))):
        pairs.append((at(zl, y, core, zh, x), at(LANDING[zl][zh], x, core, zl, y)))
    return lax.ppermute(value, HEAD + SEQ, pairs)


def on_device(query_rows, key_rows, value_rows, positions):
    tok = query_rows.shape[0]
    local_heads = query_rows.shape[1] // HD
    head = lax.axis_index(HEAD)
    key_head = (head * local_heads // (HEADS // KVH)).astype(jnp.int32).reshape(1)
    packed = pack(key_head, key_rows, value_rows, positions)
    gathered = exchange(packed, "x")
    queries = jnp.transpose(query_rows.reshape(tok, local_heads, HD), (1, 0, 2))
    attended = attend(queries, gathered, positions)
    chunk = swap(attended)
    rows = lax.all_gather(attended, "zh", axis=0, tiled=True)
    chunk, rows = lax.optimization_barrier((chunk, rows))
    landed = [[place * RING + group for place in LANDING[group]] for group in range(RING)]
    cols = lax.all_gather(chunk, ("zl", "zh"), axis=0, tiled=True, axis_index_groups=landed)
    cols, rows = lax.optimization_barrier((cols, rows))
    near = exchange(copies(cols), "y")
    pieces = [shift(rows, "x", -ahead) for ahead in (2, 1, 3)]
    near, opposite, after, before = lax.optimization_barrier((near, *pieces))
    far = swap_cores(near)
    rows = joined("x", (rows, after, opposite, before))
    near, far = (v.reshape(-1, v.shape[2]) for v in (near, far))
    core = lax.axis_index("core").astype(jnp.int32).reshape(1)
    hessian = hessian_half(core, rows, near)
    hessian = hessian_half(1 - core, rows, far, hessian)
    return attended, hessian


def solution(mesh):
    fine = Mesh(mesh.devices.reshape(4, 4, 2, 4, 4), AXES)
    placed = (P(SEQ, HEAD), P(SEQ, None), P(SEQ, None), P(SEQ))
    return jax.shard_map(
        on_device,
        mesh=fine,
        in_specs=placed,
        out_specs=(P(SEQ, HEAD), P(HEAD, SEQ)),
        check_vma=False,
    )
```

```python
import itertools

import jax
import jax.numpy as jnp
from jax import lax
from jax.experimental import pallas as pl
from jax.experimental.pallas import tpu as pltpu
from jax.sharding import Mesh
from jax.sharding import PartitionSpec as P

HEADS = 128
KVH = 8
HD = 128
RING = 4
STEPS = 2
AXES = ("zl", "y", "core", "zh", "x")
HEAD = ("zl", "y", "core")
SEQ = ("zh", "x")
VMEM = 24 * 1024 * 1024


def pack_kernel(g_ref, k_ref, v_ref, p_ref, o_ref):
    tok = k_ref.shape[0]
    p = p_ref[...]
    high = p >> 7
    row = lax.broadcasted_iota(jnp.int32, (16, tok), 0)
    both = jnp.where(row == 0, high, p - (high << 7))
    both = both.astype(jnp.float32).astype(jnp.bfloat16)
    for copy in range(o_ref.shape[0]):
        o_ref[copy, :tok] = k_ref[...]
        o_ref[copy, tok : 2 * tok] = v_ref[...]
        o_ref[copy, 2 * tok :] = both


def pack(key_head, key_rows, value_rows, positions):
    tok = key_rows.shape[0]
    return pl.pallas_call(
        pack_kernel,
        out_shape=jax.ShapeDtypeStruct((RING, 2 * tok + 16, HD), jnp.bfloat16),
        grid_spec=pltpu.PrefetchScalarGridSpec(
            num_scalar_prefetch=1,
            grid=(1,),
            in_specs=[
                pl.BlockSpec((tok, HD), lambda i, g: (0, g[0])),
                pl.BlockSpec((tok, HD), lambda i, g: (0, g[0])),
                pl.BlockSpec((1, tok), lambda i, g: (0, 0)),
            ],
            out_specs=pl.BlockSpec((RING, 2 * tok + 16, HD), lambda i, g: (0, 0, 0)),
        ),
        name="pack",
    )(key_head, key_rows, value_rows, positions.reshape(1, tok))


def attend_kernel(q_ref, kv_ref, p_ref, o_ref):
    heads, tok, _ = q_ref.shape
    spans = kv_ref.shape[0]
    keys = jnp.concatenate([kv_ref[s, :tok, :] for s in range(spans)], axis=0)
    values = jnp.concatenate([kv_ref[s, tok : 2 * tok, :] for s in range(spans)], axis=0)
    places = []
    for s in range(spans):
        both = kv_ref[s, 2 * tok :, :].astype(jnp.float32)
        places.append(both[0:1] * 128.0 + both[1:2])
    place = jnp.concatenate(places, axis=1)
    own = p_ref[...].astype(jnp.float32)
    visible = place <= own
    for h in range(heads):
        q = q_ref[h]
        scores = lax.dot_general(
            q, keys, (((1,), (1,)), ((), ())), preferred_element_type=jnp.float32
        ) * (HD ** (-0.5))
        masked = jnp.where(visible, scores, -jnp.inf)
        top = jnp.max(masked, axis=1, keepdims=True)
        weights = jnp.exp(masked - top)
        total = jnp.sum(weights, axis=1, keepdims=True)
        mixed = jnp.dot(weights.astype(jnp.bfloat16), values, preferred_element_type=jnp.float32)
        o_ref[:, h * HD : (h + 1) * HD] = (mixed / total).astype(jnp.bfloat16)


def attend(queries, gathered, positions):
    heads, tok, _ = queries.shape
    return pl.pallas_call(
        attend_kernel,
        out_shape=jax.ShapeDtypeStruct((tok, heads * HD), jnp.bfloat16),
        compiler_params=pltpu.CompilerParams(vmem_limit_bytes=VMEM),
        name="attend",
    )(queries, gathered, positions.reshape(tok, 1))


LANDING = ((0, 2, 3, 1), (1, 3, 2, 0), (3, 1, 0, 2), (2, 0, 1, 3))
CONTRACT = (((0,), (0,)), ((), ()))


def half_kernel(s_ref, rows_ref, cols_ref, *rest):
    o_ref = rest[-1]
    o_ref[...] = lax.dot_general(
        rows_ref[...], cols_ref[...], CONTRACT, preferred_element_type=jnp.float32
    )


def hessian_half(place, rows, cols, filled=None):
    depth, width = rows.shape
    half = cols.shape[1]
    specs = [
        pl.BlockSpec((depth, width), lambda i, s: (0, 0)),
        pl.BlockSpec((depth, half // STEPS), lambda i, s: (0, i)),
    ]
    args = [place, rows, cols]
    aliases = {}
    if filled is not None:
        aliases = {len(args): 0}
        specs.append(pl.BlockSpec(memory_space=pl.ANY))
        args.append(filled)
    return pl.pallas_call(
        half_kernel,
        out_shape=jax.ShapeDtypeStruct((width, 2 * half), jnp.float32),
        grid_spec=pltpu.PrefetchScalarGridSpec(
            num_scalar_prefetch=1,
            grid=(STEPS,),
            in_specs=specs,
            out_specs=pl.BlockSpec((width, half // STEPS), lambda i, s: (0, s[0] * STEPS + i)),
        ),
        input_output_aliases=aliases,
        compiler_params=pltpu.CompilerParams(vmem_limit_bytes=VMEM),
        name="hessian_half",
    )(*args)


def shift(value, axis, by):
    return lax.ppermute(value, axis, [(i, (i + by) % RING) for i in range(RING)])


def joined(axis, pieces):
    me = lax.axis_index(axis)
    depth, width = pieces[0].shape
    whole = jnp.zeros((RING * depth, width), pieces[0].dtype)
    for ahead, piece in enumerate(pieces):
        start = ((me + ahead) & (RING - 1)) * depth
        whole = lax.dynamic_update_slice(whole, piece, (start, 0))
    return whole


def copies(value):
    return jnp.broadcast_to(value[None], (RING,) + value.shape)


def swap_cores(value):
    return lax.ppermute(value, "core", [(0, 1), (1, 0)])


def exchange(value, axis):
    return lax.all_to_all(value, axis, split_axis=0, concat_axis=0, tiled=True)


def swap(value):
    at = lambda zl, y, core, zh, x: (((zl * RING + y) * 2 + core) * RING + zh) * RING + x
    pairs = []
    for zl, y, core, zh, x in itertools.product(*(range(n) for n in (RING, RING, 2, RING, RING))):
        pairs.append((at(zl, y, core, zh, x), at(LANDING[zl][zh], x, core, zl, y)))
    return lax.ppermute(value, HEAD + SEQ, pairs)


def on_device(query_rows, key_rows, value_rows, positions):
    tok = query_rows.shape[0]
    local_heads = query_rows.shape[1] // HD
    head = lax.axis_index(HEAD)
    key_head = (head * local_heads // (HEADS // KVH)).astype(jnp.int32).reshape(1)
    packed = pack(key_head, key_rows, value_rows, positions)
    gathered = exchange(packed, "x")
    queries = jnp.transpose(query_rows.reshape(tok, local_heads, HD), (1, 0, 2))
    attended = attend(queries, gathered, positions)
    chunk = swap(attended)
    rows = lax.all_gather(attended, "zh", axis=0, tiled=True)
    chunk, rows = lax.optimization_barrier((chunk, rows))
    landed = [[place * RING + group for place in LANDING[group]] for group in range(RING)]
    cols = lax.all_gather(chunk, ("zl", "zh"), axis=0, tiled=True, axis_index_groups=landed)
    cols, rows = lax.optimization_barrier((cols, rows))
    near = exchange(copies(cols), "y")
    pieces = [shift(rows, "x", -ahead) for ahead in (2, 1, 3)]
    opposite, after, before = pieces
    rows = joined("x", (rows, after, opposite, before))
    near, rows = lax.optimization_barrier((near, rows))
    far = swap_cores(near)
    near, far = (v.reshape(-1, v.shape[2]) for v in (near, far))
    core = lax.axis_index("core").astype(jnp.int32).reshape(1)
    hessian = hessian_half(core, rows, near)
    hessian = hessian_half(1 - core, rows, far, hessian)
    return attended, hessian


def solution(mesh):
    fine = Mesh(mesh.devices.reshape(4, 4, 2, 4, 4), AXES)
    placed = (P(SEQ, HEAD), P(SEQ, None), P(SEQ, None), P(SEQ))
    return jax.shard_map(
        on_device,
        mesh=fine,
        in_specs=placed,
        out_specs=(P(SEQ, HEAD), P(HEAD, SEQ)),
        check_vma=False,
    )
```

```python
import itertools

import jax
import jax.numpy as jnp
from jax import lax
from jax.experimental import pallas as pl
from jax.experimental.pallas import tpu as pltpu
from jax.sharding import Mesh
from jax.sharding import PartitionSpec as P

HEADS = 128
KVH = 8
HD = 128
RING = 4
STEPS = 2
AXES = ("zl", "y", "core", "zh", "x")
HEAD = ("zl", "y", "core")
SEQ = ("zh", "x")
VMEM = 24 * 1024 * 1024


def pack_kernel(g_ref, k_ref, v_ref, p_ref, o_ref):
    tok = k_ref.shape[0]
    p = p_ref[...]
    high = p >> 7
    row = lax.broadcasted_iota(jnp.int32, (16, tok), 0)
    both = jnp.where(row == 0, high, p - (high << 7))
    both = both.astype(jnp.float32).astype(jnp.bfloat16)
    for copy in range(o_ref.shape[0]):
        o_ref[copy, :tok] = k_ref[...]
        o_ref[copy, tok : 2 * tok] = v_ref[...]
        o_ref[copy, 2 * tok :] = both


def pack(key_head, key_rows, value_rows, positions):
    tok = key_rows.shape[0]
    return pl.pallas_call(
        pack_kernel,
        out_shape=jax.ShapeDtypeStruct((RING, 2 * tok + 16, HD), jnp.bfloat16),
        grid_spec=pltpu.PrefetchScalarGridSpec(
            num_scalar_prefetch=1,
            grid=(1,),
            in_specs=[
                pl.BlockSpec((tok, HD), lambda i, g: (0, g[0])),
                pl.BlockSpec((tok, HD), lambda i, g: (0, g[0])),
                pl.BlockSpec((1, tok), lambda i, g: (0, 0)),
            ],
            out_specs=pl.BlockSpec((RING, 2 * tok + 16, HD), lambda i, g: (0, 0, 0)),
        ),
        name="pack",
    )(key_head, key_rows, value_rows, positions.reshape(1, tok))


def attend_kernel(q_ref, kv_ref, p_ref, o_ref):
    heads, tok, _ = q_ref.shape
    spans = kv_ref.shape[0]
    keys = jnp.concatenate([kv_ref[s, :tok, :] for s in range(spans)], axis=0)
    values = jnp.concatenate([kv_ref[s, tok : 2 * tok, :] for s in range(spans)], axis=0)
    places = []
    for s in range(spans):
        both = kv_ref[s, 2 * tok :, :].astype(jnp.float32)
        places.append(both[0:1] * 128.0 + both[1:2])
    place = jnp.concatenate(places, axis=1)
    own = p_ref[...].astype(jnp.float32)
    visible = place <= own
    for h in range(heads):
        q = q_ref[h]
        scores = lax.dot_general(
            q, keys, (((1,), (1,)), ((), ())), preferred_element_type=jnp.float32
        ) * (HD ** (-0.5))
        masked = jnp.where(visible, scores, -jnp.inf)
        top = jnp.max(masked, axis=1, keepdims=True)
        weights = jnp.exp(masked - top)
        total = jnp.sum(weights, axis=1, keepdims=True)
        mixed = jnp.dot(weights.astype(jnp.bfloat16), values, preferred_element_type=jnp.float32)
        o_ref[:, h * HD : (h + 1) * HD] = (mixed / total).astype(jnp.bfloat16)


def attend(queries, gathered, positions):
    heads, tok, _ = queries.shape
    return pl.pallas_call(
        attend_kernel,
        out_shape=jax.ShapeDtypeStruct((tok, heads * HD), jnp.bfloat16),
        compiler_params=pltpu.CompilerParams(vmem_limit_bytes=VMEM),
        name="attend",
    )(queries, gathered, positions.reshape(tok, 1))


LANDING = ((0, 2, 3, 1), (1, 3, 2, 0), (3, 1, 0, 2), (2, 0, 1, 3))
CONTRACT = (((0,), (0,)), ((), ()))


def half_kernel(s_ref, rows_ref, cols_ref, *rest):
    o_ref = rest[-1]
    o_ref[...] = lax.dot_general(
        rows_ref[...], cols_ref[...], CONTRACT, preferred_element_type=jnp.float32
    )


def hessian_half(place, rows, cols, filled=None):
    depth, width = rows.shape
    half = cols.shape[1]
    specs = [
        pl.BlockSpec((depth, width), lambda i, s: (0, 0)),
        pl.BlockSpec((depth, half // STEPS), lambda i, s: (0, i)),
    ]
    args = [place, rows, cols]
    aliases = {}
    if filled is not None:
        aliases = {len(args): 0}
        specs.append(pl.BlockSpec(memory_space=pl.ANY))
        args.append(filled)
    return pl.pallas_call(
        half_kernel,
        out_shape=jax.ShapeDtypeStruct((width, 2 * half), jnp.float32),
        grid_spec=pltpu.PrefetchScalarGridSpec(
            num_scalar_prefetch=1,
            grid=(STEPS,),
            in_specs=specs,
            out_specs=pl.BlockSpec((width, half // STEPS), lambda i, s: (0, s[0] * STEPS + i)),
        ),
        input_output_aliases=aliases,
        compiler_params=pltpu.CompilerParams(vmem_limit_bytes=VMEM),
        name="hessian_half",
    )(*args)


def shift(value, axis, by):
    return lax.ppermute(value, axis, [(i, (i + by) % RING) for i in range(RING)])


def joined(axis, pieces):
    me = lax.axis_index(axis)
    depth, width = pieces[0].shape
    whole = jnp.zeros((RING * depth, width), pieces[0].dtype)
    for ahead in (0, 2, 1, 3):
        start = ((me + ahead) & (RING - 1)) * depth
        whole = lax.dynamic_update_slice(whole, pieces[ahead], (start, 0))
    return whole


def copies(value):
    return jnp.broadcast_to(value[None], (RING,) + value.shape)


def swap_cores(value):
    return lax.ppermute(value, "core", [(0, 1), (1, 0)])


def exchange(value, axis):
    return lax.all_to_all(value, axis, split_axis=0, concat_axis=0, tiled=True)


def swap(value):
    at = lambda zl, y, core, zh, x: (((zl * RING + y) * 2 + core) * RING + zh) * RING + x
    pairs = []
    for zl, y, core, zh, x in itertools.product(*(range(n) for n in (RING, RING, 2, RING, RING))):
        pairs.append((at(zl, y, core, zh, x), at(LANDING[zl][zh], x, core, zl, y)))
    return lax.ppermute(value, HEAD + SEQ, pairs)


def on_device(query_rows, key_rows, value_rows, positions):
    tok = query_rows.shape[0]
    local_heads = query_rows.shape[1] // HD
    head = lax.axis_index(HEAD)
    key_head = (head * local_heads // (HEADS // KVH)).astype(jnp.int32).reshape(1)
    packed = pack(key_head, key_rows, value_rows, positions)
    gathered = exchange(packed, "x")
    queries = jnp.transpose(query_rows.reshape(tok, local_heads, HD), (1, 0, 2))
    attended = attend(queries, gathered, positions)
    chunk = swap(attended)
    rows = lax.all_gather(attended, "zh", axis=0, tiled=True)
    chunk, rows = lax.optimization_barrier((chunk, rows))
    landed = [[place * RING + group for place in LANDING[group]] for group in range(RING)]
    cols = lax.all_gather(chunk, ("zl", "zh"), axis=0, tiled=True, axis_index_groups=landed)
    cols, rows = lax.optimization_barrier((cols, rows))
    near = exchange(copies(cols), "y")
    pieces = [shift(rows, "x", -ahead) for ahead in (2, 1, 3)]
    opposite, after, before = pieces
    rows = joined("x", (rows, after, opposite, before))
    near, rows = lax.optimization_barrier((near, rows))
    far = swap_cores(near)
    near, far = (v.reshape(-1, v.shape[2]) for v in (near, far))
    core = lax.axis_index("core").astype(jnp.int32).reshape(1)
    hessian = hessian_half(core, rows, near)
    hessian = hessian_half(1 - core, rows, far, hessian)
    return attended, hessian


def solution(mesh):
    fine = Mesh(mesh.devices.reshape(4, 4, 2, 4, 4), AXES)
    placed = (P(SEQ, HEAD), P(SEQ, None), P(SEQ, None), P(SEQ))
    return jax.shard_map(
        on_device,
        mesh=fine,
        in_specs=placed,
        out_specs=(P(SEQ, HEAD), P(HEAD, SEQ)),
        check_vma=False,
    )
```

```python
import itertools

import jax
import jax.numpy as jnp
from jax import lax
from jax.experimental import pallas as pl
from jax.experimental.pallas import tpu as pltpu
from jax.sharding import Mesh
from jax.sharding import PartitionSpec as P

HEADS = 128
KVH = 8
HD = 128
RING = 4
STEPS = 2
AXES = ("zl", "y", "core", "zh", "x")
HEAD = ("zl", "y", "core")
SEQ = ("zh", "x")
VMEM = 24 * 1024 * 1024


def pack_kernel(g_ref, k_ref, v_ref, p_ref, o_ref):
    tok = k_ref.shape[0]
    p = p_ref[...]
    high = p >> 7
    row = lax.broadcasted_iota(jnp.int32, (16, tok), 0)
    both = jnp.where(row == 0, high, p - (high << 7))
    both = both.astype(jnp.float32).astype(jnp.bfloat16)
    for copy in range(o_ref.shape[0]):
        o_ref[copy, :tok] = k_ref[...]
        o_ref[copy, tok : 2 * tok] = v_ref[...]
        o_ref[copy, 2 * tok :] = both


def pack(key_head, key_rows, value_rows, positions):
    tok = key_rows.shape[0]
    return pl.pallas_call(
        pack_kernel,
        out_shape=jax.ShapeDtypeStruct((RING, 2 * tok + 16, HD), jnp.bfloat16),
        grid_spec=pltpu.PrefetchScalarGridSpec(
            num_scalar_prefetch=1,
            grid=(1,),
            in_specs=[
                pl.BlockSpec((tok, HD), lambda i, g: (0, g[0])),
                pl.BlockSpec((tok, HD), lambda i, g: (0, g[0])),
                pl.BlockSpec((1, tok), lambda i, g: (0, 0)),
            ],
            out_specs=pl.BlockSpec((RING, 2 * tok + 16, HD), lambda i, g: (0, 0, 0)),
        ),
        name="pack",
    )(key_head, key_rows, value_rows, positions.reshape(1, tok))


def attend_kernel(q_ref, kv_ref, p_ref, o_ref):
    heads, tok, _ = q_ref.shape
    spans = kv_ref.shape[0]
    keys = jnp.concatenate([kv_ref[s, :tok, :] for s in range(spans)], axis=0)
    values = jnp.concatenate([kv_ref[s, tok : 2 * tok, :] for s in range(spans)], axis=0)
    places = []
    for s in range(spans):
        both = kv_ref[s, 2 * tok :, :].astype(jnp.float32)
        places.append(both[0:1] * 128.0 + both[1:2])
    place = jnp.concatenate(places, axis=1)
    own = p_ref[...].astype(jnp.float32)
    visible = place <= own
    for h in range(heads):
        q = q_ref[h]
        scores = lax.dot_general(
            q, keys, (((1,), (1,)), ((), ())), preferred_element_type=jnp.float32
        ) * (HD ** (-0.5))
        masked = jnp.where(visible, scores, -jnp.inf)
        top = jnp.max(masked, axis=1, keepdims=True)
        weights = jnp.exp(masked - top)
        total = jnp.sum(weights, axis=1, keepdims=True)
        mixed = jnp.dot(weights.astype(jnp.bfloat16), values, preferred_element_type=jnp.float32)
        o_ref[:, h * HD : (h + 1) * HD] = (mixed / total).astype(jnp.bfloat16)


def attend(queries, gathered, positions):
    heads, tok, _ = queries.shape
    return pl.pallas_call(
        attend_kernel,
        out_shape=jax.ShapeDtypeStruct((tok, heads * HD), jnp.bfloat16),
        compiler_params=pltpu.CompilerParams(vmem_limit_bytes=VMEM),
        name="attend",
    )(queries, gathered, positions.reshape(tok, 1))


LANDING = ((0, 2, 3, 1), (1, 3, 2, 0), (3, 1, 0, 2), (2, 0, 1, 3))
TAKEN = tuple(tuple(line.index(k) for k in range(RING)) for line in LANDING)
CONTRACT = (((0,), (0,)), ((), ()))


def half_kernel(s_ref, rows_ref, cols_ref, *rest):
    o_ref = rest[-1]
    o_ref[...] = lax.dot_general(
        rows_ref[...], cols_ref[...], CONTRACT, preferred_element_type=jnp.float32
    )


def hessian_half(place, rows, cols, filled=None):
    depth, width = rows.shape
    half = cols.shape[1]
    specs = [
        pl.BlockSpec((depth, width), lambda i, s: (0, 0)),
        pl.BlockSpec((depth, half // STEPS), lambda i, s: (0, i)),
    ]
    args = [place, rows, cols]
    aliases = {}
    if filled is not None:
        aliases = {len(args): 0}
        specs.append(pl.BlockSpec(memory_space=pl.ANY))
        args.append(filled)
    return pl.pallas_call(
        half_kernel,
        out_shape=jax.ShapeDtypeStruct((width, 2 * half), jnp.float32),
        grid_spec=pltpu.PrefetchScalarGridSpec(
            num_scalar_prefetch=1,
            grid=(STEPS,),
            in_specs=specs,
            out_specs=pl.BlockSpec((width, half // STEPS), lambda i, s: (0, s[0] * STEPS + i)),
        ),
        input_output_aliases=aliases,
        compiler_params=pltpu.CompilerParams(vmem_limit_bytes=VMEM),
        name="hessian_half",
    )(*args)


def shift(value, axis, by):
    return lax.ppermute(value, axis, [(i, (i + by) % RING) for i in range(RING)])


def shift_landed(value, ahead):
    at = lambda group, slot: LANDING[group][slot % RING] * RING + group
    pairs = [(at(g, k + ahead), at(g, k)) for g in range(RING) for k in range(RING)]
    return lax.ppermute(value, ("zl", "zh"), pairs)


def joined(me, pieces):
    depth, width = pieces[0].shape
    whole = jnp.zeros((RING * depth, width), pieces[0].dtype)
    for ahead in (0, 2, 1, 3):
        start = ((me + ahead) & (RING - 1)) * depth
        whole = lax.dynamic_update_slice(whole, pieces[ahead], (start, 0))
    return whole


def copies(value):
    return jnp.broadcast_to(value[None], (RING,) + value.shape)


def swap_cores(value):
    return lax.ppermute(value, "core", [(0, 1), (1, 0)])


def exchange(value, axis):
    return lax.all_to_all(value, axis, split_axis=0, concat_axis=0, tiled=True)


def swap(value):
    at = lambda zl, y, core, zh, x: (((zl * RING + y) * 2 + core) * RING + zh) * RING + x
    pairs = []
    for zl, y, core, zh, x in itertools.product(*(range(n) for n in (RING, RING, 2, RING, RING))):
        pairs.append((at(zl, y, core, zh, x), at(LANDING[zl][zh], x, core, zl, y)))
    return lax.ppermute(value, HEAD + SEQ, pairs)


def on_device(query_rows, key_rows, value_rows, positions):
    tok = query_rows.shape[0]
    local_heads = query_rows.shape[1] // HD
    head = lax.axis_index(HEAD)
    key_head = (head * local_heads // (HEADS // KVH)).astype(jnp.int32).reshape(1)
    packed = pack(key_head, key_rows, value_rows, positions)
    gathered = exchange(packed, "x")
    queries = jnp.transpose(query_rows.reshape(tok, local_heads, HD), (1, 0, 2))
    attended = attend(queries, gathered, positions)
    chunk = swap(attended)
    rows = lax.all_gather(attended, "zh", axis=0, tiled=True)
    chunk, rows = lax.optimization_barrier((chunk, rows))
    spot = jnp.asarray(TAKEN, jnp.int32)[lax.axis_index("zh"), lax.axis_index("zl")]
    landed = [chunk] + [shift_landed(chunk, ahead) for ahead in range(1, RING)]
    opposite = shift(rows, "x", -2)
    landed, opposite = lax.optimization_barrier((landed, opposite))
    cols = joined(spot, landed)
    near = exchange(copies(cols), "y")
    after, before = shift(rows, "x", -1), shift(rows, "x", 1)
    rows = joined(lax.axis_index("x"), (rows, after, opposite, before))
    near, rows = lax.optimization_barrier((near, rows))
    far = swap_cores(near)
    near, far = (v.reshape(-1, v.shape[2]) for v in (near, far))
    core = lax.axis_index("core").astype(jnp.int32).reshape(1)
    hessian = hessian_half(core, rows, near)
    hessian = hessian_half(1 - core, rows, far, hessian)
    return attended, hessian


def solution(mesh):
    fine = Mesh(mesh.devices.reshape(4, 4, 2, 4, 4), AXES)
    placed = (P(SEQ, HEAD), P(SEQ, None), P(SEQ, None), P(SEQ))
    return jax.shard_map(
        on_device,
        mesh=fine,
        in_specs=placed,
        out_specs=(P(SEQ, HEAD), P(HEAD, SEQ)),
        check_vma=False,
    )
```

```python
import itertools

import jax
import jax.numpy as jnp
from jax import lax
from jax.experimental import pallas as pl
from jax.experimental.pallas import tpu as pltpu
from jax.sharding import Mesh
from jax.sharding import PartitionSpec as P

HEADS = 128
KVH = 8
HD = 128
RING = 4
STEPS = 2
AXES = ("zl", "y", "core", "zh", "x")
HEAD = ("zl", "y", "core")
SEQ = ("zh", "x")
VMEM = 24 * 1024 * 1024


def pack_kernel(g_ref, k_ref, v_ref, p_ref, o_ref):
    tok = k_ref.shape[0]
    p = p_ref[...]
    high = p >> 7
    row = lax.broadcasted_iota(jnp.int32, (16, tok), 0)
    both = jnp.where(row == 0, high, p - (high << 7))
    both = both.astype(jnp.float32).astype(jnp.bfloat16)
    for copy in range(o_ref.shape[0]):
        o_ref[copy, :tok] = k_ref[...]
        o_ref[copy, tok : 2 * tok] = v_ref[...]
        o_ref[copy, 2 * tok :] = both


def pack(key_head, key_rows, value_rows, positions):
    tok = key_rows.shape[0]
    return pl.pallas_call(
        pack_kernel,
        out_shape=jax.ShapeDtypeStruct((RING, 2 * tok + 16, HD), jnp.bfloat16),
        grid_spec=pltpu.PrefetchScalarGridSpec(
            num_scalar_prefetch=1,
            grid=(1,),
            in_specs=[
                pl.BlockSpec((tok, HD), lambda i, g: (0, g[0])),
                pl.BlockSpec((tok, HD), lambda i, g: (0, g[0])),
                pl.BlockSpec((1, tok), lambda i, g: (0, 0)),
            ],
            out_specs=pl.BlockSpec((RING, 2 * tok + 16, HD), lambda i, g: (0, 0, 0)),
        ),
        name="pack",
    )(key_head, key_rows, value_rows, positions.reshape(1, tok))


def attend_kernel(q_ref, kv_ref, p_ref, o_ref):
    heads, tok, _ = q_ref.shape
    spans = kv_ref.shape[0]
    keys = jnp.concatenate([kv_ref[s, :tok, :] for s in range(spans)], axis=0)
    values = jnp.concatenate([kv_ref[s, tok : 2 * tok, :] for s in range(spans)], axis=0)
    places = []
    for s in range(spans):
        both = kv_ref[s, 2 * tok :, :].astype(jnp.float32)
        places.append(both[0:1] * 128.0 + both[1:2])
    place = jnp.concatenate(places, axis=1)
    own = p_ref[...].astype(jnp.float32)
    visible = place <= own
    for h in range(heads):
        q = q_ref[h]
        scores = lax.dot_general(
            q, keys, (((1,), (1,)), ((), ())), preferred_element_type=jnp.float32
        ) * (HD ** (-0.5))
        masked = jnp.where(visible, scores, -jnp.inf)
        top = jnp.max(masked, axis=1, keepdims=True)
        weights = jnp.exp(masked - top)
        total = jnp.sum(weights, axis=1, keepdims=True)
        mixed = jnp.dot(weights.astype(jnp.bfloat16), values, preferred_element_type=jnp.float32)
        o_ref[:, h * HD : (h + 1) * HD] = (mixed / total).astype(jnp.bfloat16)


def attend(queries, gathered, positions):
    heads, tok, _ = queries.shape
    return pl.pallas_call(
        attend_kernel,
        out_shape=jax.ShapeDtypeStruct((tok, heads * HD), jnp.bfloat16),
        compiler_params=pltpu.CompilerParams(vmem_limit_bytes=VMEM),
        name="attend",
    )(queries, gathered, positions.reshape(tok, 1))


LANDING = ((0, 2, 3, 1), (1, 3, 2, 0), (3, 1, 0, 2), (2, 0, 1, 3))
CONTRACT = (((0,), (0,)), ((), ()))


def half_kernel(s_ref, rows_ref, cols_ref, *rest):
    o_ref = rest[-1]
    o_ref[...] = lax.dot_general(
        rows_ref[...], cols_ref[...], CONTRACT, preferred_element_type=jnp.float32
    )


def hessian_half(place, rows, cols, filled=None):
    depth, width = rows.shape
    half = cols.shape[1]
    specs = [
        pl.BlockSpec((depth, width), lambda i, s: (0, 0)),
        pl.BlockSpec((depth, half // STEPS), lambda i, s: (0, i)),
    ]
    args = [place, rows, cols]
    aliases = {}
    if filled is not None:
        aliases = {len(args): 0}
        specs.append(pl.BlockSpec(memory_space=pl.ANY))
        args.append(filled)
    return pl.pallas_call(
        half_kernel,
        out_shape=jax.ShapeDtypeStruct((width, 2 * half), jnp.float32),
        grid_spec=pltpu.PrefetchScalarGridSpec(
            num_scalar_prefetch=1,
            grid=(STEPS,),
            in_specs=specs,
            out_specs=pl.BlockSpec((width, half // STEPS), lambda i, s: (0, s[0] * STEPS + i)),
        ),
        input_output_aliases=aliases,
        compiler_params=pltpu.CompilerParams(vmem_limit_bytes=VMEM),
        name="hessian_half",
    )(*args)


def shift(value, axis, by):
    return lax.ppermute(value, axis, [(i, (i + by) % RING) for i in range(RING)])


def turn(value, by):
    steps = ((0, by), (1, -by))
    pairs = [(c * RING + i, c * RING + (i + d) % RING) for c, d in steps for i in range(RING)]
    return lax.ppermute(value, ("core", "x"), pairs)


def joined(me, pieces):
    depth, width = pieces[0][1].shape
    whole = jnp.zeros((RING * depth, width), pieces[0][1].dtype)
    for ahead, piece in pieces:
        start = ((me + ahead) & (RING - 1)) * depth
        whole = lax.dynamic_update_slice(whole, piece, (start, 0))
    return whole


def copies(value):
    return jnp.broadcast_to(value[None], (RING,) + value.shape)


def swap_cores(value):
    return lax.ppermute(value, "core", [(0, 1), (1, 0)])


def exchange(value, axis):
    return lax.all_to_all(value, axis, split_axis=0, concat_axis=0, tiled=True)


def swap(value):
    at = lambda zl, y, core, zh, x: (((zl * RING + y) * 2 + core) * RING + zh) * RING + x
    pairs = []
    for zl, y, core, zh, x in itertools.product(*(range(n) for n in (RING, RING, 2, RING, RING))):
        pairs.append((at(zl, y, core, zh, x), at(LANDING[zl][zh], x, core, zl, y)))
    return lax.ppermute(value, HEAD + SEQ, pairs)


def on_device(query_rows, key_rows, value_rows, positions):
    tok = query_rows.shape[0]
    local_heads = query_rows.shape[1] // HD
    head = lax.axis_index(HEAD)
    key_head = (head * local_heads // (HEADS // KVH)).astype(jnp.int32).reshape(1)
    packed = pack(key_head, key_rows, value_rows, positions)
    gathered = exchange(packed, "x")
    queries = jnp.transpose(query_rows.reshape(tok, local_heads, HD), (1, 0, 2))
    attended = attend(queries, gathered, positions)
    chunk = swap(attended)
    rows = lax.all_gather(attended, "zh", axis=0, tiled=True)
    chunk, rows = lax.optimization_barrier((chunk, rows))
    landed = [[place * RING + group for place in LANDING[group]] for group in range(RING)]
    cols = lax.all_gather(chunk, ("zl", "zh"), axis=0, tiled=True, axis_index_groups=landed)
    cols, rows = lax.optimization_barrier((cols, rows))
    near = exchange(copies(cols), "y")
    opposite = shift(rows, "x", -2)
    one, two = turn(rows, -1), turn(rows, 1)
    step = jnp.where(lax.axis_index("core") == 0, 1, RING - 1)
    pieces = ((0, rows), (2, opposite), (step, one), (-step, two))
    rows = joined(lax.axis_index("x"), pieces)
    near, rows = lax.optimization_barrier((near, rows))
    far = swap_cores(near)
    near, far = (v.reshape(-1, v.shape[2]) for v in (near, far))
    core = lax.axis_index("core").astype(jnp.int32).reshape(1)
    hessian = hessian_half(core, rows, near)
    hessian = hessian_half(1 - core, rows, far, hessian)
    return attended, hessian


def solution(mesh):
    fine = Mesh(mesh.devices.reshape(4, 4, 2, 4, 4), AXES)
    placed = (P(SEQ, HEAD), P(SEQ, None), P(SEQ, None), P(SEQ))
    return jax.shard_map(
        on_device,
        mesh=fine,
        in_specs=placed,
        out_specs=(P(SEQ, HEAD), P(HEAD, SEQ)),
        check_vma=False,
    )
```

```python
import itertools

import jax
import jax.numpy as jnp
from jax import lax
from jax.experimental import pallas as pl
from jax.experimental.pallas import tpu as pltpu
from jax.sharding import Mesh
from jax.sharding import PartitionSpec as P

HEADS = 128
KVH = 8
HD = 128
RING = 4
STEPS = 2
AXES = ("zl", "y", "core", "zh", "x")
HEAD = ("zl", "y", "core")
SEQ = ("zh", "x")
VMEM = 24 * 1024 * 1024


def pack_kernel(g_ref, k_ref, v_ref, p_ref, o_ref):
    tok = k_ref.shape[0]
    p = p_ref[...]
    high = p >> 7
    row = lax.broadcasted_iota(jnp.int32, (16, tok), 0)
    both = jnp.where(row == 0, high, p - (high << 7))
    both = both.astype(jnp.float32).astype(jnp.bfloat16)
    for copy in range(o_ref.shape[0]):
        o_ref[copy, :tok] = k_ref[...]
        o_ref[copy, tok : 2 * tok] = v_ref[...]
        o_ref[copy, 2 * tok :] = both


def pack(key_head, key_rows, value_rows, positions):
    tok = key_rows.shape[0]
    return pl.pallas_call(
        pack_kernel,
        out_shape=jax.ShapeDtypeStruct((RING, 2 * tok + 16, HD), jnp.bfloat16),
        grid_spec=pltpu.PrefetchScalarGridSpec(
            num_scalar_prefetch=1,
            grid=(1,),
            in_specs=[
                pl.BlockSpec((tok, HD), lambda i, g: (0, g[0])),
                pl.BlockSpec((tok, HD), lambda i, g: (0, g[0])),
                pl.BlockSpec((1, tok), lambda i, g: (0, 0)),
            ],
            out_specs=pl.BlockSpec((RING, 2 * tok + 16, HD), lambda i, g: (0, 0, 0)),
        ),
        name="pack",
    )(key_head, key_rows, value_rows, positions.reshape(1, tok))


def attend_kernel(q_ref, kv_ref, p_ref, o_ref):
    heads, tok, _ = q_ref.shape
    spans = kv_ref.shape[0]
    keys = jnp.concatenate([kv_ref[s, :tok, :] for s in range(spans)], axis=0)
    values = jnp.concatenate([kv_ref[s, tok : 2 * tok, :] for s in range(spans)], axis=0)
    places = []
    for s in range(spans):
        both = kv_ref[s, 2 * tok :, :].astype(jnp.float32)
        places.append(both[0:1] * 128.0 + both[1:2])
    place = jnp.concatenate(places, axis=1)
    own = p_ref[...].astype(jnp.float32)
    visible = place <= own
    for h in range(heads):
        q = q_ref[h]
        scores = lax.dot_general(
            q, keys, (((1,), (1,)), ((), ())), preferred_element_type=jnp.float32
        ) * (HD ** (-0.5))
        masked = jnp.where(visible, scores, -jnp.inf)
        top = jnp.max(masked, axis=1, keepdims=True)
        weights = jnp.exp(masked - top)
        total = jnp.sum(weights, axis=1, keepdims=True)
        mixed = jnp.dot(weights.astype(jnp.bfloat16), values, preferred_element_type=jnp.float32)
        o_ref[:, h * HD : (h + 1) * HD] = (mixed / total).astype(jnp.bfloat16)


def attend(queries, gathered, positions):
    heads, tok, _ = queries.shape
    return pl.pallas_call(
        attend_kernel,
        out_shape=jax.ShapeDtypeStruct((tok, heads * HD), jnp.bfloat16),
        compiler_params=pltpu.CompilerParams(vmem_limit_bytes=VMEM),
        name="attend",
    )(queries, gathered, positions.reshape(tok, 1))


LANDING = ((0, 2, 3, 1), (1, 3, 2, 0), (3, 1, 0, 2), (2, 0, 1, 3))
CONTRACT = (((0,), (0,)), ((), ()))


def half_kernel(s_ref, rows_ref, cols_ref, *rest):
    o_ref = rest[-1]
    o_ref[...] = lax.dot_general(
        rows_ref[...], cols_ref[...], CONTRACT, preferred_element_type=jnp.float32
    )


def hessian_half(place, rows, cols, filled=None):
    depth, width = rows.shape
    half = cols.shape[1]
    specs = [
        pl.BlockSpec((depth, width), lambda i, s: (0, 0)),
        pl.BlockSpec((depth, half // STEPS), lambda i, s: (0, i)),
    ]
    args = [place, rows, cols]
    aliases = {}
    if filled is not None:
        aliases = {len(args): 0}
        specs.append(pl.BlockSpec(memory_space=pl.ANY))
        args.append(filled)
    return pl.pallas_call(
        half_kernel,
        out_shape=jax.ShapeDtypeStruct((width, 2 * half), jnp.float32),
        grid_spec=pltpu.PrefetchScalarGridSpec(
            num_scalar_prefetch=1,
            grid=(STEPS,),
            in_specs=specs,
            out_specs=pl.BlockSpec((width, half // STEPS), lambda i, s: (0, s[0] * STEPS + i)),
        ),
        input_output_aliases=aliases,
        compiler_params=pltpu.CompilerParams(vmem_limit_bytes=VMEM),
        name="hessian_half",
    )(*args)


def shift(value, axis, by):
    return lax.ppermute(value, axis, [(i, (i + by) % RING) for i in range(RING)])


def placed(whole, axis, ahead, piece):
    start = ((lax.axis_index(axis) + ahead) & (RING - 1)) * piece.shape[0]
    return lax.dynamic_update_slice(whole, piece, (start, 0))


def copies(value):
    return jnp.broadcast_to(value[None], (RING,) + value.shape)


def swap_cores(value):
    return lax.ppermute(value, "core", [(0, 1), (1, 0)])


def exchange(value, axis):
    return lax.all_to_all(value, axis, split_axis=0, concat_axis=0, tiled=True)


def swap(value):
    at = lambda zl, y, core, zh, x: (((zl * RING + y) * 2 + core) * RING + zh) * RING + x
    pairs = []
    for zl, y, core, zh, x in itertools.product(*(range(n) for n in (RING, RING, 2, RING, RING))):
        pairs.append((at(zl, y, core, zh, x), at(LANDING[zl][zh], x, core, zl, y)))
    return lax.ppermute(value, HEAD + SEQ, pairs)


def on_device(query_rows, key_rows, value_rows, positions):
    tok = query_rows.shape[0]
    local_heads = query_rows.shape[1] // HD
    head = lax.axis_index(HEAD)
    key_head = (head * local_heads // (HEADS // KVH)).astype(jnp.int32).reshape(1)
    packed = pack(key_head, key_rows, value_rows, positions)
    gathered = exchange(packed, "x")
    queries = jnp.transpose(query_rows.reshape(tok, local_heads, HD), (1, 0, 2))
    attended = attend(queries, gathered, positions)
    chunk = swap(attended)
    rows = lax.all_gather(attended, "zh", axis=0, tiled=True)
    chunk, rows = lax.optimization_barrier((chunk, rows))
    landed = [[place * RING + group for place in LANDING[group]] for group in range(RING)]
    cols = lax.all_gather(chunk, ("zl", "zh"), axis=0, tiled=True, axis_index_groups=landed)
    cols, rows = lax.optimization_barrier((cols, rows))
    near = exchange(copies(cols), "y")
    pieces = [shift(rows, "x", -ahead) for ahead in (2, 1, 3)]
    opposite, after, before = pieces
    whole = jnp.zeros((RING * rows.shape[0], rows.shape[1]), rows.dtype)
    for ahead, piece in ((0, rows), (2, opposite), (1, after)):
        whole = placed(whole, "x", ahead, piece)
    near, whole, before = lax.optimization_barrier((near, whole, before))
    rows = placed(whole, "x", 3, before)
    far = swap_cores(near)
    near, far = (v.reshape(-1, v.shape[2]) for v in (near, far))
    core = lax.axis_index("core").astype(jnp.int32).reshape(1)
    hessian = hessian_half(core, rows, near)
    hessian = hessian_half(1 - core, rows, far, hessian)
    return attended, hessian


def solution(mesh):
    fine = Mesh(mesh.devices.reshape(4, 4, 2, 4, 4), AXES)
    placed = (P(SEQ, HEAD), P(SEQ, None), P(SEQ, None), P(SEQ))
    return jax.shard_map(
        on_device,
        mesh=fine,
        in_specs=placed,
        out_specs=(P(SEQ, HEAD), P(HEAD, SEQ)),
        check_vma=False,
    )
```
